32 devices in a mesh: inst: 8 (over y, x, core), tp: 4 (over z).
Axes of the slice: x: 2, y: 2, z: 4, core: 2. Of those that a mesh axis runs over, the one named last changes fastest.
Arguments:
- hidden: bfloat16 [4, 256, 8192], P(None, 'inst'), may hold values from -6 to 6
- query_weight: bfloat16 [8192, 2048], P(None, 'tp'), may hold values from -0.0625 to 0.0625
- output_weight: bfloat16 [2048, 8192], P('tp'), may hold values from -0.125 to 0.125
- kv_pool: bfloat16 [768, 2, 64, 512], P('inst', None, None, 'tp'), may hold values from -620 to 620
- new_kv: bfloat16 [4, 256, 2, 512], P(None, 'inst', None, 'tp'), may hold values from -6 to 6
- lengths: int32 [256], P('inst'), may hold values from 1 to 192, as said below
- page_table: int32 [256, 3], P('inst'), may hold values from 0 to 95, as said below
- mig_req: int32 [64], P('inst'), may hold values from 0 to 31, as said below
- mig_dest: int32 [64, 1], P('inst'), may hold values from 0 to 7; in each aligned block of 8 rows (0 to 7, 8 to 15, ...) at most 2 rows name the same one
- resume: int32 [64], P('inst'), may hold values from 0 to 3
Outputs:
- home_out: bfloat16 [4, 256, 8192], P(None, 'inst', 'tp')
- arrival_out: bfloat16 [4, 128, 8192], P(None, 'inst', 'tp')
- arrival_cache: bfloat16 [128, 3, 2, 64, 512], P('inst', None, None, None, 'tp')
The draws below stay inside these ranges and needn't reach their ends.
Inputs may be any that keep to these rules, and one draw needn't show every extreme that they name: Every draw has a request with exactly 192 cached tokens; typical lengths differ between instances by up to a factor of four. `page_table`: each instance's rows together name every page number of its pool exactly once. `mig_req`: the leaving requests of one instance are distinct. `mig_dest`: among the rows of one instance, no instance is named more than 2 times.
All inputs are finite; a program needn't handle non-finite values.
Results may differ from the reference program's by a relative error of at most 0.012.
Values may be sent and summed in bfloat16 or wider, within the bound.
A program may use at most 128 MiB of HBM per device.

```python
import math
import jax
import jax.numpy as jnp
import numpy as np

D = 8192
HD = 128
GROUP = 4
STEPS = 4
PAGE = 64
CAP = 2
REQS = 32
MAXP = 3
KV_HEADS = 4
INSTANCES = 8
MIG = 8
ARRIVALS = 16
POOL = 96


def draw_kv_pool(key, part):
    key = jax.random.fold_in(key, 41)
    first = jax.random.fold_in(key, 0)
    count = INSTANCES * POOL
    shape = (count, 2, PAGE, KV_HEADS * HD)
    base = jnp.clip(jax.random.normal(first, shape, jnp.float32), -6.0, 6.0)
    return base.astype(jnp.bfloat16)


def draw_lengths(key, part):
    key = jax.random.fold_in(key, 11)
    first, second, third = jax.random.split(key, 3)
    longest = MAXP * PAGE
    load = jax.random.randint(first, (INSTANCES, 1), 1, 5)
    spread = jnp.maximum(load * longest // 4, 1)
    raw = jax.random.randint(second, (INSTANCES, REQS), 0, 1 << 20)
    values = (1 + raw % spread).reshape(-1)
    pick = jax.random.randint(third, (), 0, INSTANCES * REQS)
    marker = jnp.arange(INSTANCES * REQS, dtype=jnp.int32) == pick
    return jnp.where(marker, longest, values).astype(jnp.int32)


def draw_page_table(key, part):
    key = jax.random.fold_in(key, 23)
    keys = jax.random.split(key, INSTANCES)
    tables = jax.vmap(lambda single: jax.random.permutation(single, POOL))(keys)
    return tables.reshape(INSTANCES * REQS, MAXP).astype(jnp.int32)


def draw_mig_req(key, part):
    key = jax.random.fold_in(key, 37)
    keys = jax.random.split(key, INSTANCES)
    chosen = jax.vmap(lambda single: jax.random.permutation(single, REQS)[:MIG])(keys)
    return chosen.reshape(-1).astype(jnp.int32)


def touch_ends(array, stream_key, low, largest):
    spot = [jax.random.randint(jax.random.fold_in(stream_key, axis), (), 0, length) for axis, length in enumerate(array.shape)]
    widest = array.shape.index(max(array.shape))
    neighbour = spot[:widest] + [(spot[widest] + 1) % array.shape[widest]] + spot[widest + 1:]
    return array.at[tuple(spot)].set(low).at[tuple(neighbour)].set(largest)


def block_levels(key, dims, cuts, least, top_value):
    factor_of = 1.0
    for dim, parts in cuts:
        steps = jax.random.uniform(jax.random.fold_in(jax.random.fold_in(key, 6), dim), (parts,), jnp.float32, least / len(cuts), top_value / len(cuts))
        factor_of = factor_of * jnp.repeat(jnp.exp(steps), dims[dim] // parts).reshape((-1,) + (1,) * (len(dims) - 1 - dim))
    return factor_of


def routed_block(rng, own, number, rows, amount, top, limit, slope):
    sequence = jax.random.permutation(rng, amount)
    crowded, common = load_shares(amount, rows * top, limit, slope, True), load_shares(amount, rows * top, limit, slope, False)
    places = jnp.arange(amount)

    def named(sizes, turn):
        used = int((sizes > 0).sum())
        fixed = max(1, used // 4)
        shifted = fixed + (places - fixed + turn * (used - fixed)) % max(1, amount - fixed)
        return jnp.zeros((amount,), jnp.int32).at[sequence[jnp.where(places < fixed, places, shifted)]].set(jnp.asarray(sizes, jnp.int32))

    sizes = jnp.where(number % 4 == 0, named(crowded, number // 4), named(common, number - number // 4 - 1))
    mixed = jax.random.permutation(jax.random.fold_in(own, 3), amount)
    donor, sink = mixed[0:amount // 2 * 2:2], mixed[1:amount // 2 * 2:2]
    slack = jnp.minimum(sizes[donor] - 1, limit - sizes[sink]) // 2
    slack = jnp.where((donor == sequence[0]) | (sink == sequence[0]) | (sizes[sink] == 0), 0, jnp.maximum(slack, 0))
    shifted = jax.random.randint(jax.random.fold_in(own, 4), (amount // 2,), 0, 1 << 20) % (slack + 1)
    sizes = sizes.at[donor].add(-shifted).at[sink].add(shifted)
    labels = jnp.searchsorted(jnp.cumsum(sizes), jnp.arange(rows * top), side="right").astype(jnp.int32)
    grid = labels.reshape(top, rows).T
    grid = grid[jax.random.permutation(jax.random.fold_in(own, 1), rows)]
    turn = jax.random.randint(jax.random.fold_in(own, 2), (rows, 1), 0, top)
    return jnp.take_along_axis(grid, (jnp.arange(top)[None, :] + turn) % top, axis=1)


def load_shares(amount, total, reach, skew, full):
    portions = [(1 << 20) // math.isqrt(rank ** skew) + 1 for rank in range(1, amount + 1)]
    largest = reach if full else min(reach, max(-(-total // amount), total * portions[0] // sum(portions)))
    least = 1 if total - largest >= amount - 1 else 0
    counts, spare = [largest] + [least] * (amount - 1), total - largest - least * (amount - 1)
    while spare > 0:
        candidates = [i for i in range(1, amount) if counts[i] < largest] or [i for i in range(1, amount) if counts[i] < reach]
        pool, remaining = sum([portions[i] for i in candidates]), spare
        for i in candidates:
            more = min(reach - counts[i], max(1, remaining * portions[i] // pool), spare)
            counts[i] = counts[i] + more
            spare = spare - more
    return np.array(counts)


def scatter_about(own_key, extent, scale, reach, cuts=(), kind=jnp.bfloat16):
    values = jax.random.normal(own_key, extent, jnp.float32) * scale
    if len(cuts) > 0:
        values = block_levels(own_key, extent, cuts, -0.22, 0.18) * values
    return jnp.clip(values, min=-reach, max=reach).astype(kind)


def setup_inputs(seed: int = 0) -> dict:
    splits = jax.random.split(jax.random.key(seed), 11)
    hidden = scatter_about(splits[0], (STEPS, INSTANCES * REQS, D), 1.0, 6.0, ((1, 8),))
    query_weight = scatter_about(splits[1], (D, KV_HEADS * GROUP * HD), D ** -0.5, 0.0625, ((1, 4),))
    output_weight = scatter_about(splits[2], (KV_HEADS * GROUP * HD, D), (KV_HEADS * GROUP * HD) ** -0.5, 0.125, ((0, 4),))
    kv_pool = draw_kv_pool(jax.random.fold_in(splits[10], 71), 0)
    new_kv = scatter_about(splits[4], (STEPS, INSTANCES * REQS, 2, KV_HEADS * HD), 1.0, 6.0, ((1, 8), (3, 4)))
    lengths = draw_lengths(jax.random.fold_in(splits[10], 71), 0)
    page_table = draw_page_table(jax.random.fold_in(splits[10], 71), 0)
    mig_req = draw_mig_req(jax.random.fold_in(splits[10], 71), 0)
    mig_dest_keys = jax.random.split(jax.random.fold_in(splits[8], 1), (INSTANCES * MIG) // MIG)
    mig_dest_turns = jax.random.permutation(jax.random.fold_in(splits[8], 3), (INSTANCES * MIG) // MIG)
    mig_dest = jax.vmap(lambda own, number: routed_block(jax.random.fold_in(splits[8], 2), own, number, MIG, INSTANCES, 1, CAP, 2))(mig_dest_keys, mig_dest_turns).reshape((INSTANCES * MIG, 1))
    resume = touch_ends(jax.random.randint(splits[9], (INSTANCES * MIG,), 0, STEPS), jax.random.fold_in(splits[9], 1), 0, STEPS - 1).astype(jnp.int32)
    return {"hidden": hidden, "query_weight": query_weight, "output_weight": output_weight, "kv_pool": kv_pool, "new_kv": new_kv, "lengths": lengths, "page_table": page_table, "mig_req": mig_req, "mig_dest": mig_dest, "resume": resume}


ROPE_BASE = 500000.0


def rotate(query, position):
    half = query.shape[-1] // 2
    inverse = ROPE_BASE ** (-jnp.arange(half, dtype=jnp.float32) * 2.0 / query.shape[-1])
    angles = position.astype(jnp.float32)[..., None] * inverse
    angles = jnp.concatenate([angles, angles], axis=-1)
    turned = jnp.concatenate([-query[..., half:], query[..., :half]], axis=-1)
    return query * jnp.cos(angles) + turned * jnp.sin(angles)


def attend(query, pages, length, fresh):
    count = pages.shape[0]
    depth = query.shape[-1]
    steps_n = query.shape[0]
    keys = pages[:, :, 0].reshape(count, -1, depth).astype(jnp.float32)
    values = pages[:, :, 1].reshape(count, -1, depth).astype(jnp.float32)
    query_wide = query.astype(jnp.float32)
    fresh_wide = fresh.astype(jnp.float32)
    scale = depth ** -0.5
    older = jnp.einsum("sbgd,bld->bsgl", query_wide, keys) * scale
    newer = jnp.einsum("sbgd,ubd->bsgu", query_wide, fresh_wide[:, :, 0]) * scale
    live = jnp.arange(keys.shape[1], dtype=jnp.int32)[None, :] < length[:, None]
    older = jnp.where(live[:, None, None, :], older, -1e30)
    step_ids = jnp.arange(steps_n, dtype=jnp.int32)
    causal = step_ids[None, :] <= step_ids[:, None]
    newer = jnp.where(causal[None, :, None, :], newer, -1e30)
    top = jnp.maximum(jnp.max(older, axis=-1), jnp.max(newer, axis=-1))[..., None]
    older_w = jnp.exp(older - top)
    newer_w = jnp.exp(newer - top)
    total = (jnp.sum(older_w, axis=-1) + jnp.sum(newer_w, axis=-1))[..., None]
    older_p = (older_w / total).astype(jnp.bfloat16).astype(jnp.float32)
    newer_p = (newer_w / total).astype(jnp.bfloat16).astype(jnp.float32)
    result = jnp.einsum("bsgl,bld->sbgd", older_p, values)
    result = result + jnp.einsum("bsgu,ubd->sbgd", newer_p, fresh_wide[:, :, 1])
    return result.astype(jnp.bfloat16).reshape(steps_n, count, -1)


def reference(hidden, query_weight, output_weight, kv_pool, new_kv, lengths, page_table, mig_req, mig_dest, resume):
    steps_n, rows, width = hidden.shape
    heads_kv = kv_pool.shape[-1] // HD
    query = jnp.dot(hidden.reshape(-1, width), query_weight, preferred_element_type=jnp.float32)
    query = query.reshape(steps_n, rows, heads_kv, GROUP, HD)
    position = lengths[None, :] + jnp.arange(steps_n, dtype=jnp.int32)[:, None]
    rotated = rotate(query, position[:, :, None, None]).astype(jnp.bfloat16)
    owner = jnp.arange(rows, dtype=jnp.int32) // REQS
    global_pages = (owner[:, None] * POOL + page_table).astype(jnp.int32)
    raw_pages = kv_pool[global_pages]
    pages = raw_pages.reshape(rows, MAXP, 2, PAGE, heads_kv, HD)
    fresh = new_kv.reshape(steps_n, rows, 2, heads_kv, HD)
    per_head = jax.vmap(attend, in_axes=(2, 4, None, 3), out_axes=2)(rotated, pages, lengths, fresh)
    attended = per_head.reshape(steps_n, rows, -1)
    leaving = INSTANCES * MIG
    home_index = ((jnp.arange(leaving, dtype=jnp.int32) // MIG) * REQS + mig_req).astype(jnp.int32)
    moved = jnp.full((rows,), steps_n, jnp.int32).at[home_index].set(resume)
    step_ids = jnp.arange(steps_n, dtype=jnp.int32)[:, None]
    zero_rows = jnp.zeros_like(attended)
    home_rows = jnp.where((step_ids < moved[None, :])[:, :, None], attended, zero_rows)
    home_out = jnp.dot(home_rows.reshape(-1, home_rows.shape[-1]), output_weight, preferred_element_type=jnp.float32)
    home_out = home_out.reshape(steps_n, rows, -1).astype(jnp.bfloat16)
    dest = mig_dest[:, 0].reshape(INSTANCES, MIG)
    order = jnp.arange(MIG, dtype=jnp.int32)
    same = dest[:, :, None] == dest[:, None, :]
    earlier = order[None, None, :] < order[None, :, None]
    rank = jnp.sum((same & earlier).astype(jnp.int32), axis=2)
    source = jnp.arange(INSTANCES, dtype=jnp.int32)[:, None]
    slot = (dest * ARRIVALS + source * CAP + rank).reshape(-1).astype(jnp.int32)
    arrival_cache = jnp.zeros((INSTANCES * ARRIVALS,) + raw_pages.shape[1:], raw_pages.dtype).at[slot].set(raw_pages[home_index])
    taken = attended[:, home_index]
    carried = jnp.where((step_ids >= resume[None, :])[:, :, None], taken, jnp.zeros_like(taken))
    arrival_rows = jnp.zeros((steps_n, INSTANCES * ARRIVALS, attended.shape[-1]), attended.dtype).at[:, slot].set(carried)
    arrival_out = jnp.dot(arrival_rows.reshape(-1, arrival_rows.shape[-1]), output_weight, preferred_element_type=jnp.float32)
    arrival_out = arrival_out.reshape(steps_n, INSTANCES * ARRIVALS, -1).astype(jnp.bfloat16)
    return home_out, arrival_out, arrival_cache
```

```python
import jax
import jax.numpy as jnp
from jax import lax
from jax.sharding import PartitionSpec as P

HD = 128
GROUP = 4
CAP = 2


ROPE_BASE = 500000.0


def rotate(query, position):
    half = query.shape[-1] // 2
    inverse = ROPE_BASE ** (-jnp.arange(half, dtype=jnp.float32) * 2.0 / query.shape[-1])
    angles = position.astype(jnp.float32)[..., None] * inverse
    angles = jnp.concatenate([angles, angles], axis=-1)
    turned = jnp.concatenate([-query[..., half:], query[..., :half]], axis=-1)
    return query * jnp.cos(angles) + turned * jnp.sin(angles)


def attend(query, pages, length, fresh):
    count = pages.shape[0]
    depth = query.shape[-1]
    steps_n = query.shape[0]
    keys = pages[:, :, 0].reshape(count, -1, depth)
    values = pages[:, :, 1].reshape(count, -1, depth)
    scale = depth ** (-0.5)
    older = jnp.einsum("sbgd,bld->bsgl", query, keys, preferred_element_type=jnp.float32) * scale
    newer = (
        jnp.einsum("sbgd,ubd->bsgu", query, fresh[:, :, 0], preferred_element_type=jnp.float32)
        * scale
    )
    live = jnp.arange(keys.shape[1], dtype=jnp.int32)[None, :] < length[:, None]
    older = jnp.where(live[:, None, None, :], older, -1e30)
    step_ids = jnp.arange(steps_n, dtype=jnp.int32)
    causal = step_ids[None, :] <= step_ids[:, None]
    newer = jnp.where(causal[None, :, None, :], newer, -1e30)
    top = jnp.maximum(jnp.max(older, axis=-1), jnp.max(newer, axis=-1))[..., None]
    older_w = jnp.exp(older - top)
    newer_w = jnp.exp(newer - top)
    total = (jnp.sum(older_w, axis=-1) + jnp.sum(newer_w, axis=-1))[..., None]
    older_p = (older_w / total).astype(jnp.bfloat16)
    newer_p = (newer_w / total).astype(jnp.bfloat16)
    result = jnp.einsum("bsgl,bld->sbgd", older_p, values, preferred_element_type=jnp.float32)
    result = result + jnp.einsum(
        "bsgu,ubd->sbgd", newer_p, fresh[:, :, 1], preferred_element_type=jnp.float32
    )
    return result.astype(jnp.bfloat16).reshape(steps_n, count, -1)


def local(
    hidden,
    query_weight,
    output_weight,
    kv_pool,
    new_kv,
    lengths,
    page_table,
    mig_req,
    mig_dest,
    resume,
):
    steps_n, local_rows, width = hidden.shape
    instances = lax.axis_size("inst")
    leaving = mig_req.shape[0]
    order = jnp.arange(leaving, dtype=jnp.int32)
    dest = mig_dest[:, 0]
    same = dest[None, :] == dest[:, None]
    earlier = order[None, :] < order[:, None]
    rank = jnp.sum((same & earlier).astype(jnp.int32), axis=1)
    slot = dest * CAP + rank
    slot_ids = jnp.arange(instances * CAP, dtype=jnp.int32)
    chosen = (slot_ids[:, None] == slot[None, :]).astype(jnp.int32)
    slot_request = jnp.sum(chosen * mig_req[None, :], axis=1)
    filled = jnp.sum(chosen, axis=1)
    slot_resume = jnp.where(filled > 0, jnp.sum(chosen * resume[None, :], axis=1), steps_n)
    slot_table = jnp.sum(chosen[:, :, None] * page_table[mig_req][None], axis=1)
    slot_pages = jnp.where(
        (filled > 0)[:, None, None, None, None], kv_pool[slot_table], jnp.zeros((), kv_pool.dtype)
    )
    got_pages = lax.all_to_all(slot_pages, "inst", split_axis=0, concat_axis=0, tiled=True)
    query = jnp.dot(hidden.reshape(-1, width), query_weight, preferred_element_type=jnp.float32)
    query = query.reshape(steps_n, local_rows, GROUP, HD)
    position = lengths[None, :] + jnp.arange(steps_n, dtype=jnp.int32)[:, None]
    rotated = rotate(query, position[:, :, None]).astype(jnp.bfloat16)
    pages = kv_pool[page_table]
    attended = attend(rotated, pages, lengths, new_kv)
    hit = mig_req[:, None] == jnp.arange(local_rows, dtype=jnp.int32)[None, :]
    moved = jnp.min(jnp.where(hit, resume[:, None], steps_n), axis=0)
    step_ids = jnp.arange(steps_n, dtype=jnp.int32)[:, None]
    partial_sum = jnp.dot(
        attended.reshape(-1, attended.shape[-1]), output_weight, preferred_element_type=jnp.float32
    ).astype(jnp.bfloat16)
    tp = lax.axis_size("tp")
    share = width // tp
    parts = jnp.transpose(partial_sum.reshape(-1, tp, share), (1, 0, 2))
    got = lax.all_to_all(parts, "tp", split_axis=0, concat_axis=0, tiled=True)
    mine = jnp.sum(got.astype(jnp.float32), axis=0).astype(jnp.bfloat16)
    mine = mine.reshape(steps_n, local_rows, share)
    zero = jnp.zeros((), jnp.bfloat16)
    home = jnp.where((step_ids < moved[None, :])[:, :, None], mine, zero)
    leaver = jnp.where((step_ids >= slot_resume[None, :])[:, :, None], mine[:, slot_request], zero)
    arrival = lax.all_to_all(leaver, "inst", split_axis=1, concat_axis=1, tiled=True)
    return (home, arrival, got_pages)


def solution(mesh):
    in_specs = (
        P(None, "inst", None),
        P(None, "tp"),
        P("tp", None),
        P("inst", None, None, "tp"),
        P(None, "inst", None, "tp"),
        P("inst"),
        P("inst", None),
        P("inst"),
        P("inst", None),
        P("inst"),
    )
    out_specs = (P(None, "inst", "tp"), P(None, "inst", "tp"), P("inst", None, None, None, "tp"))
    return jax.shard_map(local, mesh=mesh, in_specs=in_specs, out_specs=out_specs, check_vma=False)
```

```python
import functools

import jax
import jax.numpy as jnp
from jax import lax
from jax.experimental import pallas as pl
from jax.experimental.pallas import tpu as pltpu
from jax.sharding import PartitionSpec as P

HD = 128
GROUP = 4
CAP = 2


ROPE_BASE = 500000.0


def rotate(query, position):
    half = query.shape[-1] // 2
    inverse = ROPE_BASE ** (-jnp.arange(half, dtype=jnp.float32) * 2.0 / query.shape[-1])
    angles = position.astype(jnp.float32)[..., None] * inverse
    angles = jnp.concatenate([angles, angles], axis=-1)
    turned = jnp.concatenate([-query[..., half:], query[..., :half]], axis=-1)
    return query * jnp.cos(angles) + turned * jnp.sin(angles)


def attend(query, pages, length, fresh):
    count = pages.shape[0]
    depth = query.shape[-1]
    steps_n = query.shape[0]
    keys = pages[:, :, 0].reshape(count, -1, depth)
    values = pages[:, :, 1].reshape(count, -1, depth)
    scale = depth ** (-0.5)
    older = jnp.einsum("sbgd,bld->bsgl", query, keys, preferred_element_type=jnp.float32) * scale
    newer = (
        jnp.einsum("sbgd,ubd->bsgu", query, fresh[:, :, 0], preferred_element_type=jnp.float32)
        * scale
    )
    live = jnp.arange(keys.shape[1], dtype=jnp.int32)[None, :] < length[:, None]
    older = jnp.where(live[:, None, None, :], older, -1e30)
    step_ids = jnp.arange(steps_n, dtype=jnp.int32)
    causal = step_ids[None, :] <= step_ids[:, None]
    newer = jnp.where(causal[None, :, None, :], newer, -1e30)
    top = jnp.maximum(jnp.max(older, axis=-1), jnp.max(newer, axis=-1))[..., None]
    older_w = jnp.exp(older - top)
    newer_w = jnp.exp(newer - top)
    total = (jnp.sum(older_w, axis=-1) + jnp.sum(newer_w, axis=-1))[..., None]
    older_p = (older_w / total).astype(jnp.bfloat16)
    newer_p = (newer_w / total).astype(jnp.bfloat16)
    result = jnp.einsum("bsgl,bld->sbgd", older_p, values, preferred_element_type=jnp.float32)
    result = result + jnp.einsum(
        "bsgu,ubd->sbgd", newer_p, fresh[:, :, 1], preferred_element_type=jnp.float32
    )
    return result.astype(jnp.bfloat16).reshape(steps_n, count, -1)


MESH = pl.DeviceIdType.MESH


def project_kernel(
    n, ni, chunks, att_ref, w_ref, keep_ref, sel_ref, pages_ref,
    home_ref, arrive_ref, got_ref,
    w_buf, part, up_in, down_in, up_out, down_out, leave,
    w_sem, up_send, up_recv, down_send, down_recv, page_send, page_recv, row_send, row_recv, own_sem,
):
    z = lax.axis_index("tp")
    me = lax.axis_index("inst")
    width = part.shape[2]
    low = z < n // 2

    def block_of(k):
        return jnp.where(low, n - 1 - k // chunks, k // chunks)

    def w_copy(k):
        column = (block_of(k) * chunks + k % chunks) * width
        return pltpu.make_async_copy(
            w_ref.at[:, pl.ds(pl.multiple_of(column, width), width)], w_buf.at[k], w_sem.at[k]
        )

    for k in range(n * chunks):
        w_copy(k).start()

    barrier = pltpu.get_barrier_semaphore()
    for k in range(1, ni):
        pl.semaphore_signal(
            barrier, inc=1, device_id={"inst": lax.rem(me + k, ni)}, device_id_type=MESH
        )

    @pl.when(z > 0)
    def _():
        pl.semaphore_signal(barrier, inc=1, device_id={"tp": z - 1}, device_id_type=MESH)

    @pl.when(z < n - 1)
    def _():
        pl.semaphore_signal(barrier, inc=1, device_id={"tp": z + 1}, device_id_type=MESH)

    pl.semaphore_wait(barrier, ni - 1 + (z > 0).astype(jnp.int32) + (z < n - 1).astype(jnp.int32))

    cap = pages_ref.shape[0] // ni

    def page_copy(k):
        to = lax.rem(me + k, ni)
        return pltpu.make_async_remote_copy(
            src_ref=pages_ref.at[pl.ds(to * cap, cap)],
            dst_ref=got_ref.at[pl.ds(me * cap, cap)],
            send_sem=page_send.at[k],
            recv_sem=page_recv.at[k],
            device_id={"inst": to},
            device_id_type=MESH,
        )

    own_pages = pltpu.make_async_copy(
        pages_ref.at[pl.ds(me * cap, cap)], got_ref.at[pl.ds(me * cap, cap)], own_sem.at[0]
    )

    def up_copy(j):
        return pltpu.make_async_remote_copy(
            src_ref=up_out.at[j], dst_ref=up_in.at[j],
            send_sem=up_send.at[j], recv_sem=up_recv.at[j],
            device_id={"tp": jnp.minimum(z + 1, n - 1)}, device_id_type=MESH,
        )

    def down_copy(j):
        return pltpu.make_async_remote_copy(
            src_ref=down_out.at[j], dst_ref=down_in.at[j],
            send_sem=down_send.at[j], recv_sem=down_recv.at[j],
            device_id={"tp": jnp.maximum(z - 1, 0)}, device_id_type=MESH,
        )

    def compute(k, carry):
        w_copy(k).wait()
        value = jnp.dot(att_ref[...], w_buf[k], preferred_element_type=jnp.float32)
        part[block_of(k) * chunks + k % chunks] = value

        @pl.when((z == 0) & (k < (n - 1) * chunks))
        def _():
            up_out[k] = value.astype(jnp.bfloat16)
            up_copy(k).start()

        @pl.when((z == n - 1) & (k < (n - 1) * chunks))
        def _():
            down_out[k] = value.astype(jnp.bfloat16)
            down_copy(k).start()

        return carry

    lax.fori_loop(0, n * chunks, compute, 0)
    for k in range(1, ni):
        page_copy(k).start()
    own_pages.start()

    up_lag = jnp.maximum(z - 1, 0)
    down_lag = jnp.maximum(n - 2 - z, 0)

    def relay(j, carry):
        ju = j - up_lag
        jd = j - down_lag

        @pl.when((z > 0) & (ju >= 0) & (ju < (n - z) * chunks))
        def _():
            up_copy(ju).wait_recv()
            spot = (n - 1 - ju // chunks) * chunks + ju % chunks
            value = part[spot] + up_in[ju].astype(jnp.float32)

            @pl.when(ju < (n - 1 - z) * chunks)
            def _():
                up_out[ju] = value.astype(jnp.bfloat16)
                up_copy(ju).start()

            @pl.when(ju >= (n - 1 - z) * chunks)
            def _():
                part[spot] = value

        @pl.when((z < n - 1) & (jd >= 0) & (jd < (z + 1) * chunks))
        def _():
            down_copy(jd).wait_recv()
            value = part[jd] + down_in[jd].astype(jnp.float32)

            @pl.when(jd < z * chunks)
            def _():
                down_out[jd] = value.astype(jnp.bfloat16)
                down_copy(jd).start()

            @pl.when(jd >= z * chunks)
            def _():
                part[jd] = value

        return carry

    lax.fori_loop(0, (n - 1) * chunks + n - 2, relay, 0)

    half = chunks // 2
    for c in range(half):
        pieces = []
        for d in (c, c + half):
            mine = part[z * chunks + d].astype(jnp.bfloat16)
            home_ref[:, d * width:(d + 1) * width] = jnp.where(
                keep_ref[...] > 0, mine, jnp.zeros_like(mine)
            )
            rows = jnp.dot(sel_ref[...], mine, preferred_element_type=jnp.float32)
            pieces.append(rows.reshape(ni, -1, width))
        leave[:, :, c * width:(c + 1) * width] = jnp.concatenate(pieces, axis=1).astype(jnp.bfloat16)

    def row_copy(k):
        to = lax.rem(me + k, ni)
        return pltpu.make_async_remote_copy(
            src_ref=leave.at[to],
            dst_ref=arrive_ref.at[me],
            send_sem=row_send.at[k],
            recv_sem=row_recv.at[k],
            device_id={"inst": to},
            device_id_type=MESH,
        )

    own_rows = pltpu.make_async_copy(leave.at[me], arrive_ref.at[me], own_sem.at[1])
    for k in range(1, ni):
        row_copy(k).start()
    own_rows.start()

    def drain(j, carry):
        @pl.when((z < n - 1) & (j < (n - 1 - z) * chunks))
        def _():
            up_copy(j).wait_send()

        @pl.when((z > 0) & (j < z * chunks))
        def _():
            down_copy(j).wait_send()

        return carry

    lax.fori_loop(0, (n - 1) * chunks, drain, 0)
    for k in range(1, ni):
        page_copy(k).wait()
    own_pages.wait()
    for k in range(1, ni):
        row_copy(k).wait()
    own_rows.wait()


def project(attended, output_weight, keep, select, pages):
    n = lax.axis_size("tp")
    ni = lax.axis_size("inst")
    rows, inner = attended.shape
    width = output_weight.shape[1]
    share = width // n
    chunk = min(512, share // 2)
    chunks = share // chunk
    hops = (n - 1) * chunks
    slot_rows = select.shape[0] // ni
    vmem = pl.BlockSpec(memory_space=pltpu.VMEM)
    hbm = pl.BlockSpec(memory_space=pl.ANY)
    relay = pltpu.VMEM((hops, rows, chunk), jnp.bfloat16)
    dma = pltpu.SemaphoreType.DMA
    return pl.pallas_call(
        functools.partial(project_kernel, n, ni, chunks),
        out_shape=(
            jax.ShapeDtypeStruct((rows, share), jnp.bfloat16),
            jax.ShapeDtypeStruct((ni, 2 * slot_rows, share // 2), jnp.bfloat16),
            jax.ShapeDtypeStruct(pages.shape, pages.dtype),
        ),
        in_specs=[vmem, hbm, vmem, vmem, hbm],
        out_specs=(vmem, hbm, hbm),
        scratch_shapes=[
            pltpu.VMEM((n * chunks, inner, chunk), jnp.bfloat16),
            pltpu.VMEM((n * chunks, rows, chunk), jnp.float32),
            relay, relay, relay, relay,
            pltpu.VMEM((ni, 2 * slot_rows, share // 2), jnp.bfloat16),
            dma((n * chunks,)),
            dma((hops,)), dma((hops,)), dma((hops,)), dma((hops,)),
            dma((ni,)), dma((ni,)), dma((ni,)), dma((ni,)), dma((2,)),
        ],
        compiler_params=pltpu.CompilerParams(
            collective_id=0, has_side_effects=True, vmem_limit_bytes=40 * 1024 * 1024
        ),
        cost_estimate=pl.CostEstimate(
            flops=2 * rows * inner * width,
            bytes_accessed=2 * inner * width + 4 * pages.size,
            transcendentals=0,
        ),
    )(attended, output_weight, keep, select, pages)


def local(
    hidden,
    query_weight,
    output_weight,
    kv_pool,
    new_kv,
    lengths,
    page_table,
    mig_req,
    mig_dest,
    resume,
):
    steps_n, local_rows, width = hidden.shape
    instances = lax.axis_size("inst")
    leaving = mig_req.shape[0]
    order = jnp.arange(leaving, dtype=jnp.int32)
    dest = mig_dest[:, 0]
    same = dest[None, :] == dest[:, None]
    earlier = order[None, :] < order[:, None]
    rank = jnp.sum((same & earlier).astype(jnp.int32), axis=1)
    slot = dest * CAP + rank
    slot_ids = jnp.arange(instances * CAP, dtype=jnp.int32)
    chosen = (slot_ids[:, None] == slot[None, :]).astype(jnp.int32)
    slot_request = jnp.sum(chosen * mig_req[None, :], axis=1)
    filled = jnp.sum(chosen, axis=1)
    slot_resume = jnp.where(filled > 0, jnp.sum(chosen * resume[None, :], axis=1), steps_n)
    slot_table = jnp.sum(chosen[:, :, None] * page_table[mig_req][None], axis=1)
    slot_pages = jnp.where(
        (filled > 0)[:, None, None, None, None], kv_pool[slot_table], jnp.zeros((), kv_pool.dtype)
    )
    query = jnp.dot(hidden.reshape(-1, width), query_weight, preferred_element_type=jnp.float32)
    query = query.reshape(steps_n, local_rows, GROUP, HD)
    position = lengths[None, :] + jnp.arange(steps_n, dtype=jnp.int32)[:, None]
    rotated = rotate(query, position[:, :, None]).astype(jnp.bfloat16)
    pages = kv_pool[page_table]
    attended = attend(rotated, pages, lengths, new_kv)
    hit = mig_req[:, None] == jnp.arange(local_rows, dtype=jnp.int32)[None, :]
    moved = jnp.min(jnp.where(hit, resume[:, None], steps_n), axis=0)
    step_ids = jnp.arange(steps_n, dtype=jnp.int32)[:, None]
    keep = (step_ids < moved[None, :]).astype(jnp.int32).reshape(-1, 1)
    goes = step_ids[None] >= slot_resume[:, None, None]
    row_ids = jnp.arange(local_rows, dtype=jnp.int32)
    picked = (slot_request[:, None] == row_ids[None, :]) & (filled > 0)[:, None]
    same_step = step_ids == jnp.arange(steps_n, dtype=jnp.int32)[None, :]
    select = (goes & same_step[None])[:, :, :, None] & picked[:, None, None, :]
    select = select.astype(jnp.bfloat16).reshape(instances * CAP * steps_n, steps_n * local_rows)
    home, arrive, got_pages = project(
        attended.reshape(-1, attended.shape[-1]), output_weight, keep, select, slot_pages
    )
    home = home.reshape(steps_n, local_rows, -1)
    arrive = arrive.reshape(instances, 2, CAP, steps_n, -1)
    arrival = jnp.transpose(arrive, (3, 0, 2, 1, 4)).reshape(steps_n, instances * CAP, -1)
    return (home, arrival, got_pages)


def solution(mesh):
    in_specs = (
        P(None, "inst", None),
        P(None, "tp"),
        P("tp", None),
        P("inst", None, None, "tp"),
        P(None, "inst", None, "tp"),
        P("inst"),
        P("inst", None),
        P("inst"),
        P("inst", None),
        P("inst"),
    )
    out_specs = (P(None, "inst", "tp"), P(None, "inst", "tp"), P("inst", None, None, None, "tp"))
    return jax.shard_map(local, mesh=mesh, in_specs=in_specs, out_specs=out_specs, check_vma=False)
```

```python
import functools

import jax
import jax.numpy as jnp
from jax import lax
from jax.experimental import pallas as pl
from jax.experimental.pallas import tpu as pltpu
from jax.sharding import PartitionSpec as P

HD = 128
GROUP = 4
CAP = 2


ROPE_BASE = 500000.0


def turns(position, depth):
    half = depth // 2
    inverse = ROPE_BASE ** (-jnp.arange(half, dtype=jnp.float32) * 2.0 / depth)
    angles = position.astype(jnp.float32)[:, None] * inverse
    cosine = jnp.cos(angles)
    sine = jnp.sin(angles)
    return jnp.concatenate([cosine, cosine], axis=1), jnp.concatenate([-sine, sine], axis=1)


def attend_kernel(
    lengths, table, slot_table, filled, hidden_ref, wq_ref, pool_ref, fresh_ref, cos_ref, sin_ref,
    att_ref, slots_ref,
    h_buf, w_buf, pool, query, result, h_sem, w_sem, pool_sem,
):
    steps = w_buf.shape[0]
    depth = w_buf.shape[1]
    requests, pairs, hd = query.shape
    groups = att_ref.shape[1] // hd
    steps_n = pairs // groups
    page = pool.shape[2]
    maxp = table.shape[1]

    def h_copy(k):
        return pltpu.make_async_copy(
            hidden_ref.at[:, pl.ds(k * depth, depth)], h_buf.at[k], h_sem.at[k]
        )

    def w_copy(k):
        return pltpu.make_async_copy(wq_ref.at[pl.ds(k * depth, depth)], w_buf.at[k], w_sem.at[k])

    pool_copy = pltpu.make_async_copy(pool_ref, pool, pool_sem)
    for k in range(steps):
        h_copy(k).start()
        w_copy(k).start()
    pool_copy.start()
    total = jnp.zeros(att_ref.shape, jnp.float32)
    for k in range(steps):
        h_copy(k).wait()
        w_copy(k).wait()
        total = total + jnp.dot(h_buf[k], w_buf[k], preferred_element_type=jnp.float32)
    for g in range(groups):
        head = total[:, g * hd:(g + 1) * hd]
        head = head * cos_ref[...] + pltpu.roll(head, hd // 2, 1) * sin_ref[...]
        for s in range(steps_n):
            query[:, s * groups + g, :] = head[s * requests:(s + 1) * requests]
    pool_copy.wait()

    old = maxp * page
    span = old + page
    column = lax.broadcasted_iota(jnp.int32, (pairs, span), 1)
    step = lax.broadcasted_iota(jnp.int32, (pairs, span), 0) // groups
    newer = (column >= old) & (column - old <= step)
    scale = hd ** (-0.5)
    empty = jnp.zeros((page - fresh_ref.shape[2], hd), jnp.bfloat16)

    def one(r):
        pages = [pool[table[r, p]] for p in range(maxp)]
        fresh = fresh_ref[r]
        keys = jnp.concatenate([x[0] for x in pages] + [fresh[0], empty], axis=0)
        scores = lax.dot_general(
            query[r].astype(jnp.bfloat16), keys, (((1,), (1,)), ((), ())),
            preferred_element_type=jnp.float32,
        ) * scale
        live = newer | (column < lengths[r])
        scores = jnp.where(live, scores, -1e30)
        weight = jnp.exp(scores - jnp.max(scores, axis=1, keepdims=True))
        probs = (weight / jnp.sum(weight, axis=1, keepdims=True)).astype(jnp.bfloat16)
        values = jnp.concatenate([x[1] for x in pages] + [fresh[1], empty], axis=0)
        result[r] = jnp.dot(probs, values, preferred_element_type=jnp.float32)

    unroll = 8

    def several(i, carry):
        for k in range(unroll):
            one(i * unroll + k)
        return carry

    lax.fori_loop(0, requests // unroll, several, 0)

    def slot(i, carry):
        for p in range(maxp):
            chosen = pool[slot_table[i, p]]
            slots_ref[i, p] = jnp.where(filled[i] > 0, chosen, jnp.zeros_like(chosen))
        return carry

    lax.fori_loop(0, slots_ref.shape[0], slot, 0)
    for s in range(steps_n):
        for g in range(groups):
            att_ref[s * requests:(s + 1) * requests, g * hd:(g + 1) * hd] = result[
                :, s * groups + g, :
            ].astype(jnp.bfloat16)


def attend(hidden, query_weight, kv_pool, new_kv, cosine, sine, lengths, table, slot_table, filled):
    steps_n, requests, width = hidden.shape
    columns = query_weight.shape[1]
    hd = kv_pool.shape[-1]
    pairs = steps_n * (columns // hd)
    fresh = jnp.transpose(new_kv, (1, 2, 0, 3))
    fresh = jnp.pad(fresh, ((0, 0), (0, 0), (0, 16 - steps_n), (0, 0)))
    cuts = 8
    depth = width // cuts
    vmem = pl.BlockSpec(memory_space=pltpu.VMEM)
    smem = pl.BlockSpec(memory_space=pltpu.SMEM)
    hbm = pl.BlockSpec(memory_space=pl.ANY)
    slots = slot_table.shape[0]
    return pl.pallas_call(
        attend_kernel,
        out_shape=(
            jax.ShapeDtypeStruct((steps_n * requests, columns), jnp.bfloat16),
            jax.ShapeDtypeStruct((slots, table.shape[1]) + kv_pool.shape[1:], kv_pool.dtype),
        ),
        in_specs=[smem] * 4 + [hbm, hbm, hbm, vmem, vmem, vmem],
        out_specs=(vmem, vmem),
        scratch_shapes=[
            pltpu.VMEM((cuts, steps_n * requests, depth), jnp.bfloat16),
            pltpu.VMEM((cuts, depth, columns), jnp.bfloat16),
            pltpu.VMEM(kv_pool.shape, kv_pool.dtype),
            pltpu.VMEM((requests, pairs, hd), jnp.float32),
            pltpu.VMEM((requests, pairs, hd), jnp.float32),
            pltpu.SemaphoreType.DMA((cuts,)),
            pltpu.SemaphoreType.DMA((cuts,)),
            pltpu.SemaphoreType.DMA,
        ],
        compiler_params=pltpu.CompilerParams(vmem_limit_bytes=40 * 1024 * 1024),
    )(
        lengths, table, slot_table, filled, hidden.reshape(-1, width), query_weight, kv_pool, fresh,
        cosine, sine,
    )


MESH = pl.DeviceIdType.MESH


def project_kernel(
    n, ni, chunks, att_ref, w_ref, keep_ref, sel_ref, pages_ref,
    home_ref, arrive_ref, got_ref,
    w_buf, part, up_in, down_in, up_out, down_out, leave,
    w_sem, up_send, up_recv, down_send, down_recv, page_send, page_recv, row_send, row_recv, own_sem,
):
    z = lax.axis_index("tp")
    me = lax.axis_index("inst")
    width = part.shape[2]
    low = z < n // 2

    def block_of(k):
        return jnp.where(low, n - 1 - k // chunks, k // chunks)

    def w_copy(k):
        column = (block_of(k) * chunks + k % chunks) * width
        return pltpu.make_async_copy(
            w_ref.at[:, pl.ds(pl.multiple_of(column, width), width)], w_buf.at[k], w_sem.at[k]
        )

    for k in range(n * chunks):
        w_copy(k).start()

    barrier = pltpu.get_barrier_semaphore()
    for k in range(1, ni):
        pl.semaphore_signal(
            barrier, inc=1, device_id={"inst": lax.rem(me + k, ni)}, device_id_type=MESH
        )

    @pl.when(z > 0)
    def _():
        pl.semaphore_signal(barrier, inc=1, device_id={"tp": z - 1}, device_id_type=MESH)

    @pl.when(z < n - 1)
    def _():
        pl.semaphore_signal(barrier, inc=1, device_id={"tp": z + 1}, device_id_type=MESH)

    pl.semaphore_wait(barrier, ni - 1 + (z > 0).astype(jnp.int32) + (z < n - 1).astype(jnp.int32))

    cap = pages_ref.shape[0] // ni

    def page_copy(k):
        to = lax.rem(me + k, ni)
        return pltpu.make_async_remote_copy(
            src_ref=pages_ref.at[pl.ds(to * cap, cap)],
            dst_ref=got_ref.at[pl.ds(me * cap, cap)],
            send_sem=page_send.at[k],
            recv_sem=page_recv.at[k],
            device_id={"inst": to},
            device_id_type=MESH,
        )

    own_pages = pltpu.make_async_copy(
        pages_ref.at[pl.ds(me * cap, cap)], got_ref.at[pl.ds(me * cap, cap)], own_sem.at[0]
    )

    def up_copy(j):
        return pltpu.make_async_remote_copy(
            src_ref=up_out.at[j], dst_ref=up_in.at[j],
            send_sem=up_send.at[j], recv_sem=up_recv.at[j],
            device_id={"tp": jnp.minimum(z + 1, n - 1)}, device_id_type=MESH,
        )

    def down_copy(j):
        return pltpu.make_async_remote_copy(
            src_ref=down_out.at[j], dst_ref=down_in.at[j],
            send_sem=down_send.at[j], recv_sem=down_recv.at[j],
            device_id={"tp": jnp.maximum(z - 1, 0)}, device_id_type=MESH,
        )

    def compute(k, carry):
        w_copy(k).wait()
        value = jnp.dot(att_ref[...], w_buf[k], preferred_element_type=jnp.float32)
        part[block_of(k) * chunks + k % chunks] = value

        @pl.when((z == 0) & (k < (n - 1) * chunks))
        def _():
            up_out[k] = value.astype(jnp.bfloat16)
            up_copy(k).start()

        @pl.when((z == n - 1) & (k < (n - 1) * chunks))
        def _():
            down_out[k] = value.astype(jnp.bfloat16)
            down_copy(k).start()

        return carry

    lax.fori_loop(0, n * chunks, compute, 0)
    for k in range(1, ni):
        page_copy(k).start()
    own_pages.start()

    up_lag = jnp.maximum(z - 1, 0)
    down_lag = jnp.maximum(n - 2 - z, 0)

    def relay(j, carry):
        ju = j - up_lag
        jd = j - down_lag

        @pl.when((z > 0) & (ju >= 0) & (ju < (n - z) * chunks))
        def _():
            up_copy(ju).wait_recv()
            spot = (n - 1 - ju // chunks) * chunks + ju % chunks
            value = part[spot] + up_in[ju].astype(jnp.float32)

            @pl.when(ju < (n - 1 - z) * chunks)
            def _():
                up_out[ju] = value.astype(jnp.bfloat16)
                up_copy(ju).start()

            @pl.when(ju >= (n - 1 - z) * chunks)
            def _():
                part[spot] = value

        @pl.when((z < n - 1) & (jd >= 0) & (jd < (z + 1) * chunks))
        def _():
            down_copy(jd).wait_recv()
            value = part[jd] + down_in[jd].astype(jnp.float32)

            @pl.when(jd < z * chunks)
            def _():
                down_out[jd] = value.astype(jnp.bfloat16)
                down_copy(jd).start()

            @pl.when(jd >= z * chunks)
            def _():
                part[jd] = value

        return carry

    lax.fori_loop(0, (n - 1) * chunks + n - 2, relay, 0)

    half = chunks // 2
    for c in range(half):
        pieces = []
        for d in (c, c + half):
            mine = part[z * chunks + d].astype(jnp.bfloat16)
            home_ref[:, d * width:(d + 1) * width] = jnp.where(
                keep_ref[...] > 0, mine, jnp.zeros_like(mine)
            )
            rows = jnp.dot(sel_ref[...], mine, preferred_element_type=jnp.float32)
            pieces.append(rows.reshape(ni, -1, width))
        leave[:, :, c * width:(c + 1) * width] = jnp.concatenate(pieces, axis=1).astype(jnp.bfloat16)

    def row_copy(k):
        to = lax.rem(me + k, ni)
        return pltpu.make_async_remote_copy(
            src_ref=leave.at[to],
            dst_ref=arrive_ref.at[me],
            send_sem=row_send.at[k],
            recv_sem=row_recv.at[k],
            device_id={"inst": to},
            device_id_type=MESH,
        )

    own_rows = pltpu.make_async_copy(leave.at[me], arrive_ref.at[me], own_sem.at[1])
    for k in range(1, ni):
        row_copy(k).start()
    own_rows.start()

    def drain(j, carry):
        @pl.when((z < n - 1) & (j < (n - 1 - z) * chunks))
        def _():
            up_copy(j).wait_send()

        @pl.when((z > 0) & (j < z * chunks))
        def _():
            down_copy(j).wait_send()

        return carry

    lax.fori_loop(0, (n - 1) * chunks, drain, 0)
    for k in range(1, ni):
        page_copy(k).wait()
    own_pages.wait()
    for k in range(1, ni):
        row_copy(k).wait()
    own_rows.wait()


def project(attended, output_weight, keep, select, pages):
    n = lax.axis_size("tp")
    ni = lax.axis_size("inst")
    rows, inner = attended.shape
    width = output_weight.shape[1]
    share = width // n
    chunk = min(512, share // 2)
    chunks = share // chunk
    hops = (n - 1) * chunks
    slot_rows = select.shape[0] // ni
    vmem = pl.BlockSpec(memory_space=pltpu.VMEM)
    hbm = pl.BlockSpec(memory_space=pl.ANY)
    relay = pltpu.VMEM((hops, rows, chunk), jnp.bfloat16)
    dma = pltpu.SemaphoreType.DMA
    return pl.pallas_call(
        functools.partial(project_kernel, n, ni, chunks),
        out_shape=(
            jax.ShapeDtypeStruct((rows, share), jnp.bfloat16),
            jax.ShapeDtypeStruct((ni, 2 * slot_rows, share // 2), jnp.bfloat16),
            jax.ShapeDtypeStruct(pages.shape, pages.dtype),
        ),
        in_specs=[vmem, hbm, vmem, vmem, hbm],
        out_specs=(vmem, hbm, hbm),
        scratch_shapes=[
            pltpu.VMEM((n * chunks, inner, chunk), jnp.bfloat16),
            pltpu.VMEM((n * chunks, rows, chunk), jnp.float32),
            relay, relay, relay, relay,
            pltpu.VMEM((ni, 2 * slot_rows, share // 2), jnp.bfloat16),
            dma((n * chunks,)),
            dma((hops,)), dma((hops,)), dma((hops,)), dma((hops,)),
            dma((ni,)), dma((ni,)), dma((ni,)), dma((ni,)), dma((2,)),
        ],
        compiler_params=pltpu.CompilerParams(
            collective_id=0, has_side_effects=True, vmem_limit_bytes=40 * 1024 * 1024
        ),
        cost_estimate=pl.CostEstimate(
            flops=2 * rows * inner * width,
            bytes_accessed=2 * inner * width + 4 * pages.size,
            transcendentals=0,
        ),
    )(attended, output_weight, keep, select, pages)


def local(
    hidden,
    query_weight,
    output_weight,
    kv_pool,
    new_kv,
    lengths,
    page_table,
    mig_req,
    mig_dest,
    resume,
):
    steps_n, local_rows, width = hidden.shape
    instances = lax.axis_size("inst")
    leaving = mig_req.shape[0]
    order = jnp.arange(leaving, dtype=jnp.int32)
    dest = mig_dest[:, 0]
    same = dest[None, :] == dest[:, None]
    earlier = order[None, :] < order[:, None]
    rank = jnp.sum((same & earlier).astype(jnp.int32), axis=1)
    slot = dest * CAP + rank
    slot_ids = jnp.arange(instances * CAP, dtype=jnp.int32)
    chosen = (slot_ids[:, None] == slot[None, :]).astype(jnp.int32)
    slot_request = jnp.sum(chosen * mig_req[None, :], axis=1)
    filled = jnp.sum(chosen, axis=1)
    slot_resume = jnp.where(filled > 0, jnp.sum(chosen * resume[None, :], axis=1), steps_n)
    slot_table = jnp.sum(chosen[:, :, None] * page_table[mig_req][None], axis=1)
    position = lengths[None, :] + jnp.arange(steps_n, dtype=jnp.int32)[:, None]
    cosine, sine = turns(position.reshape(-1), HD)
    attended, slot_pages = attend(
        hidden, query_weight, kv_pool, new_kv, cosine, sine, lengths, page_table, slot_table, filled
    )
    hit = mig_req[:, None] == jnp.arange(local_rows, dtype=jnp.int32)[None, :]
    moved = jnp.min(jnp.where(hit, resume[:, None], steps_n), axis=0)
    step_ids = jnp.arange(steps_n, dtype=jnp.int32)[:, None]
    keep = (step_ids < moved[None, :]).astype(jnp.int32).reshape(-1, 1)
    goes = step_ids[None] >= slot_resume[:, None, None]
    row_ids = jnp.arange(local_rows, dtype=jnp.int32)
    picked = (slot_request[:, None] == row_ids[None, :]) & (filled > 0)[:, None]
    same_step = step_ids == jnp.arange(steps_n, dtype=jnp.int32)[None, :]
    select = (goes & same_step[None])[:, :, :, None] & picked[:, None, None, :]
    select = select.astype(jnp.bfloat16).reshape(instances * CAP * steps_n, steps_n * local_rows)
    home, arrive, got_pages = project(
        attended, output_weight, keep, select, slot_pages
    )
    home = home.reshape(steps_n, local_rows, -1)
    arrive = arrive.reshape(instances, 2, CAP, steps_n, -1)
    arrival = jnp.transpose(arrive, (3, 0, 2, 1, 4)).reshape(steps_n, instances * CAP, -1)
    return (home, arrival, got_pages)


def solution(mesh):
    in_specs = (
        P(None, "inst", None),
        P(None, "tp"),
        P("tp", None),
        P("inst", None, None, "tp"),
        P(None, "inst", None, "tp"),
        P("inst"),
        P("inst", None),
        P("inst"),
        P("inst", None),
        P("inst"),
    )
    out_specs = (P(None, "inst", "tp"), P(None, "inst", "tp"), P("inst", None, None, None, "tp"))
    return jax.shard_map(local, mesh=mesh, in_specs=in_specs, out_specs=out_specs, check_vma=False)
```

```python
import functools

import jax
import jax.numpy as jnp
from jax import lax
from jax.experimental import pallas as pl
from jax.experimental.pallas import tpu as pltpu
from jax.sharding import PartitionSpec as P

HD = 128
CAP = 2
HALVES = 2


ROPE_BASE = 500000.0

MESH = pl.DeviceIdType.MESH


def turns(position, depth):
    half = depth // 2
    inverse = ROPE_BASE ** (-jnp.arange(half, dtype=jnp.float32) * 2.0 / depth)
    angles = position.astype(jnp.float32)[:, None] * inverse
    cosine = jnp.cos(angles)
    sine = jnp.sin(angles)
    return jnp.concatenate([cosine, cosine], axis=1), jnp.concatenate([-sine, sine], axis=1)


def layer_kernel(
    n, ni, chunks,
    lengths, table, mig_req, mig_dest, resume,
    hidden_ref, wq_ref, pool_ref, wo_ref, fresh_ref, cos_ref, sin_ref,
    home_ref, arrive_ref, got_ref,
    h_buf, wq_buf, pool, wo_buf, query, result, att, part, up_in, down_in, up_out, down_out,
    slots, select, leave,
    h_sem, wq_sem, pool_sem, wo_sem,
    up_send, up_recv, down_send, down_recv, page_send, page_recv, row_send, row_recv, own_sem,
):
    z = lax.axis_index("tp")
    me = lax.axis_index("inst")
    cuts, depth, columns = wq_buf.shape
    requests, pairs, hd = query.shape
    groups = columns // hd
    steps_n = pairs // groups
    page = pool.shape[2]
    maxp = table.shape[0]
    leaving = mig_req.shape[0]
    some = requests // HALVES
    rows, width = part.shape[2:]
    hops = (n - 1) * chunks
    low = z < n // 2

    def h_copy(k):
        return pltpu.make_async_copy(
            hidden_ref.at[:, pl.ds(k * depth, depth)], h_buf.at[k], h_sem.at[k]
        )

    def wq_copy(k):
        return pltpu.make_async_copy(
            wq_ref.at[pl.ds(k * depth, depth)], wq_buf.at[k], wq_sem.at[k]
        )

    def block_of(k):
        return jnp.where(low, n - 1 - k // chunks, k // chunks)

    def wo_copy(k):
        column = (block_of(k) * chunks + k % chunks) * width
        return pltpu.make_async_copy(
            wo_ref.at[:, pl.ds(pl.multiple_of(column, width), width)], wo_buf.at[k], wo_sem.at[k]
        )

    pool_copy = pltpu.make_async_copy(pool_ref, pool, pool_sem)
    pool_copy.start()
    for k in range(cuts):
        h_copy(k).start()
        wq_copy(k).start()
    for k in range(n * chunks):
        wo_copy(k).start()

    barrier = pltpu.get_barrier_semaphore()
    for k in range(1, ni):
        pl.semaphore_signal(
            barrier, inc=1, device_id={"inst": lax.rem(me + k, ni)}, device_id_type=MESH
        )

    @pl.when(z > 0)
    def _():
        pl.semaphore_signal(barrier, inc=1, device_id={"tp": z - 1}, device_id_type=MESH)

    @pl.when(z < n - 1)
    def _():
        pl.semaphore_signal(barrier, inc=1, device_id={"tp": z + 1}, device_id_type=MESH)

    slot_rows = CAP * steps_n
    shape = (slot_rows, HALVES * rows)
    slot_row = lax.broadcasted_iota(jnp.int32, shape, 0)
    row = lax.broadcasted_iota(jnp.int32, shape, 1)
    slot_step = slot_row % steps_n
    row_request = (row // rows) * some + row % some
    row_step = (row % rows) // some

    pool_copy.wait()

    def fill(d, carry):
        count = jnp.int32(0)
        who = [jnp.int32(-1) for _ in range(CAP)]
        start = [jnp.int32(steps_n) for _ in range(CAP)]
        for k in range(leaving):
            match = mig_dest[k] == d
            for c in range(CAP):
                take = match & (count == c)
                who[c] = jnp.where(take, mig_req[k], who[c])
                start[c] = jnp.where(take, resume[k], start[c])
            count = count + match.astype(jnp.int32)
        chosen = jnp.full(shape, -1, jnp.int32)
        first = jnp.full(shape, steps_n, jnp.int32)
        for c in range(CAP):
            chosen = jnp.where(slot_row // steps_n == c, who[c], chosen)
            first = jnp.where(slot_row // steps_n == c, start[c], first)
            for p in range(maxp):
                pages = pool[table[p, jnp.maximum(who[c], 0)]]
                slots[d * CAP + c, p] = jnp.where(who[c] >= 0, pages, jnp.zeros_like(pages))
        hit = (row_request == chosen) & (row_step == slot_step) & (slot_step >= first)
        select[d] = hit.astype(jnp.float32)
        return carry

    lax.fori_loop(0, ni, fill, 0)

    pl.semaphore_wait(barrier, ni - 1 + (z > 0).astype(jnp.int32) + (z < n - 1).astype(jnp.int32))

    def page_copy(k):
        to = lax.rem(me + k, ni)
        return pltpu.make_async_remote_copy(
            src_ref=slots.at[pl.ds(to * CAP, CAP)],
            dst_ref=got_ref.at[pl.ds(me * CAP, CAP)],
            send_sem=page_send.at[k],
            recv_sem=page_recv.at[k],
            device_id={"inst": to},
            device_id_type=MESH,
        )

    own_pages = pltpu.make_async_copy(
        slots.at[pl.ds(me * CAP, CAP)], got_ref.at[pl.ds(me * CAP, CAP)], own_sem.at[0]
    )
    for k in range(1, ni):
        page_copy(k).start()
    own_pages.start()

    total = jnp.zeros((h_buf.shape[1], columns), jnp.float32)
    for k in range(cuts):
        h_copy(k).wait()
        wq_copy(k).wait()
        total = total + jnp.dot(h_buf[k], wq_buf[k], preferred_element_type=jnp.float32)
    for g in range(groups):
        head = total[:, g * hd:(g + 1) * hd]
        head = head * cos_ref[...] + pltpu.roll(head, hd // 2, 1) * sin_ref[...]
        for s in range(steps_n):
            query[:, s * groups + g, :] = head[s * requests:(s + 1) * requests]

    old = maxp * page
    span = old + page
    column = lax.broadcasted_iota(jnp.int32, (pairs, span), 1)
    step = lax.broadcasted_iota(jnp.int32, (pairs, span), 0) // groups
    newer = (column >= old) & (column - old <= step)
    scale = hd ** (-0.5)
    empty = jnp.zeros((page - fresh_ref.shape[2], hd), jnp.bfloat16)

    def one(r):
        pages = [pool[table[p, r]] for p in range(maxp)]
        fresh = fresh_ref[r]
        keys = jnp.concatenate([x[0] for x in pages] + [fresh[0], empty], axis=0)
        scores = lax.dot_general(
            query[r].astype(jnp.bfloat16), keys, (((1,), (1,)), ((), ())),
            preferred_element_type=jnp.float32,
        ) * scale
        live = newer | (column < lengths[r])
        scores = jnp.where(live, scores, -1e30)
        weight = jnp.exp(scores - jnp.max(scores, axis=1, keepdims=True))
        probs = (weight / jnp.sum(weight, axis=1, keepdims=True)).astype(jnp.bfloat16)
        values = jnp.concatenate([x[1] for x in pages] + [fresh[1], empty], axis=0)
        result[r] = jnp.dot(probs, values, preferred_element_type=jnp.float32)

    def up_copy(j):
        return pltpu.make_async_remote_copy(
            src_ref=up_out.at[j], dst_ref=up_in.at[j],
            send_sem=up_send.at[j], recv_sem=up_recv.at[j],
            device_id={"tp": jnp.minimum(z + 1, n - 1)}, device_id_type=MESH,
        )

    def down_copy(j):
        return pltpu.make_async_remote_copy(
            src_ref=down_out.at[j], dst_ref=down_in.at[j],
            send_sem=down_send.at[j], recv_sem=down_recv.at[j],
            device_id={"tp": jnp.maximum(z - 1, 0)}, device_id_type=MESH,
        )

    unroll = 8
    for h in range(HALVES):

        def several(i, carry, h=h):
            for k in range(unroll):
                one(h * some + i * unroll + k)
            return carry

        lax.fori_loop(0, some // unroll, several, 0)
        for s in range(steps_n):
            for g in range(groups):
                att[h, s * some:(s + 1) * some, g * hd:(g + 1) * hd] = result[
                    h * some:(h + 1) * some, s * groups + g, :
                ].astype(jnp.bfloat16)

        def compute(k, carry, h=h):
            if h == 0:
                wo_copy(k).wait()
            value = jnp.dot(att[h], wo_buf[k], preferred_element_type=jnp.float32)
            part[h, block_of(k) * chunks + k % chunks] = value

            @pl.when((z == 0) & (k < hops))
            def _():
                up_out[h * hops + k] = value.astype(jnp.bfloat16)
                up_copy(h * hops + k).start()

            @pl.when((z == n - 1) & (k < hops))
            def _():
                down_out[h * hops + k] = value.astype(jnp.bfloat16)
                down_copy(h * hops + k).start()

            return carry

        lax.fori_loop(0, n * chunks, compute, 0)

    up_lag = jnp.maximum(z - 1, 0)
    down_lag = jnp.maximum(n - 2 - z, 0)
    for h in range(HALVES):

        def relay(j, carry, h=h):
            ju = j - up_lag
            jd = j - down_lag

            @pl.when((z > 0) & (ju >= 0) & (ju < (n - z) * chunks))
            def _():
                up_copy(h * hops + ju).wait_recv()
                spot = (n - 1 - ju // chunks) * chunks + ju % chunks
                value = part[h, spot] + up_in[h * hops + ju].astype(jnp.float32)

                @pl.when(ju < (n - 1 - z) * chunks)
                def _():
                    up_out[h * hops + ju] = value.astype(jnp.bfloat16)
                    up_copy(h * hops + ju).start()

                @pl.when(ju >= (n - 1 - z) * chunks)
                def _():
                    part[h, spot] = value

            @pl.when((z < n - 1) & (jd >= 0) & (jd < (z + 1) * chunks))
            def _():
                down_copy(h * hops + jd).wait_recv()
                value = part[h, jd] + down_in[h * hops + jd].astype(jnp.float32)

                @pl.when(jd < z * chunks)
                def _():
                    down_out[h * hops + jd] = value.astype(jnp.bfloat16)
                    down_copy(h * hops + jd).start()

                @pl.when(jd >= z * chunks)
                def _():
                    part[h, jd] = value

            return carry

        lax.fori_loop(0, hops + n - 2, relay, 0)

    selection = select[...].reshape(ni * slot_rows, HALVES * rows).astype(jnp.bfloat16)
    lane_row = lax.broadcasted_iota(jnp.int32, (rows, hd), 0)
    half = chunks // 2
    stays = []
    for h in range(HALVES):
        kept = jnp.ones((rows, hd), jnp.int32)
        for k in range(leaving):
            gone = (lane_row % some + h * some == mig_req[k]) & (lane_row // some >= resume[k])
            kept = jnp.where(gone, 0, kept)
        stays.append(jnp.concatenate([kept] * (width // hd), axis=1))
    for c in range(half):
        pieces = []
        for d in (c, c + half):
            mines = []
            for h in range(HALVES):
                mine = part[h, z * chunks + d].astype(jnp.bfloat16)
                mines.append(mine)
                kept = jnp.where(stays[h] > 0, mine.astype(jnp.float32), 0.0).astype(jnp.bfloat16)
                for s in range(steps_n):
                    home_ref[
                        s * requests + h * some:s * requests + (h + 1) * some,
                        d * width:(d + 1) * width,
                    ] = kept[s * some:(s + 1) * some]
            moved = jnp.dot(
                selection, jnp.concatenate(mines, axis=0), preferred_element_type=jnp.float32
            )
            pieces.append(moved.reshape(ni, slot_rows, width))
        leave[:, :, c * width:(c + 1) * width] = jnp.concatenate(pieces, axis=1).astype(jnp.bfloat16)

    def row_copy(k):
        to = lax.rem(me + k, ni)
        return pltpu.make_async_remote_copy(
            src_ref=leave.at[to],
            dst_ref=arrive_ref.at[me],
            send_sem=row_send.at[k],
            recv_sem=row_recv.at[k],
            device_id={"inst": to},
            device_id_type=MESH,
        )

    own_rows = pltpu.make_async_copy(leave.at[me], arrive_ref.at[me], own_sem.at[1])
    for k in range(1, ni):
        row_copy(k).start()
    own_rows.start()

    for h in range(HALVES):

        def drain(j, carry, h=h):
            @pl.when((z < n - 1) & (j < (n - 1 - z) * chunks))
            def _():
                up_copy(h * hops + j).wait_send()

            @pl.when((z > 0) & (j < z * chunks))
            def _():
                down_copy(h * hops + j).wait_send()

            return carry

        lax.fori_loop(0, hops, drain, 0)
    for k in range(1, ni):
        page_copy(k).wait()
    own_pages.wait()
    for k in range(1, ni):
        row_copy(k).wait()
    own_rows.wait()


def local(
    hidden,
    query_weight,
    output_weight,
    kv_pool,
    new_kv,
    lengths,
    page_table,
    mig_req,
    mig_dest,
    resume,
):
    steps_n, requests, width = hidden.shape
    n = lax.axis_size("tp")
    ni = lax.axis_size("inst")
    columns = query_weight.shape[1]
    pairs = steps_n * (columns // HD)
    maxp = page_table.shape[1]
    all_rows = steps_n * requests
    rows = all_rows // HALVES
    share = output_weight.shape[1] // n
    chunk = min(1024, share // 2)
    chunks = share // chunk
    hops = (n - 1) * chunks
    slot_rows = CAP * steps_n
    position = lengths[None, :] + jnp.arange(steps_n, dtype=jnp.int32)[:, None]
    cosine, sine = turns(position.reshape(-1), HD)
    fresh = jnp.transpose(new_kv, (1, 2, 0, 3))
    fresh = jnp.pad(fresh, ((0, 0), (0, 0), (0, 16 - steps_n), (0, 0)))
    cuts = 8
    vmem = pl.BlockSpec(memory_space=pltpu.VMEM)
    smem = pl.BlockSpec(memory_space=pltpu.SMEM)
    hbm = pl.BlockSpec(memory_space=pl.ANY)
    relay = pltpu.VMEM((HALVES * hops, rows, chunk), jnp.bfloat16)
    dma = pltpu.SemaphoreType.DMA
    bf16, f32 = jnp.bfloat16, jnp.float32
    slot_shape = (ni * CAP, maxp) + kv_pool.shape[1:]
    home, arrive, got_pages = pl.pallas_call(
        functools.partial(layer_kernel, n, ni, chunks),
        out_shape=(
            jax.ShapeDtypeStruct((all_rows, share), bf16),
            jax.ShapeDtypeStruct((ni, 2 * slot_rows, share // 2), bf16),
            jax.ShapeDtypeStruct(slot_shape, bf16),
        ),
        in_specs=[smem] * 5 + [hbm] * 4 + [vmem] * 3,
        out_specs=(vmem, hbm, hbm),
        scratch_shapes=[
            pltpu.VMEM((cuts, all_rows, width // cuts), bf16),
            pltpu.VMEM((cuts, width // cuts, columns), bf16),
            pltpu.VMEM(kv_pool.shape, bf16),
            pltpu.VMEM((n * chunks, columns, chunk), bf16),
            pltpu.VMEM((requests, pairs, HD), f32),
            pltpu.VMEM((requests, pairs, HD), f32),
            pltpu.VMEM((HALVES, rows, columns), bf16),
            pltpu.VMEM((HALVES, n * chunks, rows, chunk), f32),
            relay, relay, relay, relay,
            pltpu.VMEM(slot_shape, bf16),
            pltpu.VMEM((ni, slot_rows, all_rows), f32),
            pltpu.VMEM((ni, 2 * slot_rows, share // 2), bf16),
            dma((cuts,)), dma((cuts,)), dma, dma((n * chunks,)),
            dma((HALVES * hops,)), dma((HALVES * hops,)), dma((HALVES * hops,)), dma((HALVES * hops,)),
            dma((ni,)), dma((ni,)), dma((ni,)), dma((ni,)), dma((2,)),
        ],
        compiler_params=pltpu.CompilerParams(
            collective_id=0, has_side_effects=True, vmem_limit_bytes=60 * 1024 * 1024
        ),
    )(
        lengths, page_table.T, mig_req, mig_dest.reshape(-1), resume,
        hidden.reshape(-1, width), query_weight, kv_pool, output_weight, fresh, cosine, sine,
    )
    home = home.reshape(steps_n, requests, -1)
    arrive = arrive.reshape(ni, 2, CAP, steps_n, -1)
    arrival = jnp.transpose(arrive, (3, 0, 2, 1, 4)).reshape(steps_n, ni * CAP, -1)
    return (home, arrival, got_pages)


def solution(mesh):
    in_specs = (
        P(None, "inst", None),
        P(None, "tp"),
        P("tp", None),
        P("inst", None, None, "tp"),
        P(None, "inst", None, "tp"),
        P("inst"),
        P("inst", None),
        P("inst"),
        P("inst", None),
        P("inst"),
    )
    out_specs = (P(None, "inst", "tp"), P(None, "inst", "tp"), P("inst", None, None, None, "tp"))
    return jax.shard_map(local, mesh=mesh, in_specs=in_specs, out_specs=out_specs, check_vma=False)
```

```python
import functools

import jax
import jax.numpy as jnp
from jax import lax
from jax.experimental import pallas as pl
from jax.experimental.pallas import tpu as pltpu
from jax.sharding import PartitionSpec as P

HD = 128
CAP = 2
HALVES = 2


ROPE_BASE = 500000.0

MESH = pl.DeviceIdType.MESH


def turns(position, depth):
    half = depth // 2
    inverse = ROPE_BASE ** (-jnp.arange(half, dtype=jnp.float32) * 2.0 / depth)
    angles = position.astype(jnp.float32)[:, None] * inverse
    cosine = jnp.cos(angles)
    sine = jnp.sin(angles)
    return jnp.concatenate([cosine, cosine], axis=1), jnp.concatenate([-sine, sine], axis=1)


def layer_kernel(
    n, ni, chunks,
    lengths, table, mig_req, mig_dest, resume,
    hidden_ref, wq_ref, pool_ref, wo_ref, fresh_ref, cos_ref, sin_ref,
    home_ref, arrive_ref, got_ref,
    h_buf, wq_buf, pool, wo_buf, query, result, att, part, up_in, down_in, up_out, down_out,
    slots, select, leave, landed, fresh,
    h_sem, wq_sem, pool_sem, wo_sem,
    up_send, up_recv, down_send, down_recv, page_send, page_recv, row_send, row_recv, own_sem,
):
    z = lax.axis_index("tp")
    me = lax.axis_index("inst")
    cuts, depth, columns = wq_buf.shape
    requests, pairs, hd = query.shape
    groups = columns // hd
    steps_n = pairs // groups
    page = pool.shape[2]
    maxp = table.shape[0]
    leaving = mig_req.shape[0]
    some = requests // HALVES
    rows, width = part.shape[2:]
    hops = (n - 1) * chunks
    low = z < n // 2

    def h_copy(k):
        return pltpu.make_async_copy(
            hidden_ref.at[:, pl.ds(k * depth, depth)], h_buf.at[k], h_sem.at[k]
        )

    def wq_copy(k):
        return pltpu.make_async_copy(
            wq_ref.at[pl.ds(k * depth, depth)], wq_buf.at[k], wq_sem.at[k]
        )

    def block_of(k):
        return jnp.where(low, n - 1 - k // chunks, k // chunks)

    def wo_copy(k):
        column = (block_of(k) * chunks + k % chunks) * width
        return pltpu.make_async_copy(
            wo_ref.at[:, pl.ds(pl.multiple_of(column, width), width)], wo_buf.at[k], wo_sem.at[k]
        )

    pool_copy = pltpu.make_async_copy(pool_ref, pool, pool_sem)
    pool_copy.start()
    for k in range(cuts):
        h_copy(k).start()
        wq_copy(k).start()
    for k in range(n * chunks):
        wo_copy(k).start()

    barrier = pltpu.get_barrier_semaphore()
    for k in range(1, ni):
        pl.semaphore_signal(
            barrier, inc=1, device_id={"inst": lax.rem(me + k, ni)}, device_id_type=MESH
        )

    @pl.when(z > 0)
    def _():
        pl.semaphore_signal(barrier, inc=1, device_id={"tp": z - 1}, device_id_type=MESH)

    @pl.when(z < n - 1)
    def _():
        pl.semaphore_signal(barrier, inc=1, device_id={"tp": z + 1}, device_id_type=MESH)

    slot_rows = CAP * steps_n
    shape = (slot_rows, HALVES * rows)
    slot_row = lax.broadcasted_iota(jnp.int32, shape, 0)
    row = lax.broadcasted_iota(jnp.int32, shape, 1)
    slot_step = slot_row % steps_n
    row_request = (row // rows) * some + row % some
    row_step = (row % rows) // some

    pool_copy.wait()

    def fill(d, carry):
        count = jnp.int32(0)
        who = [jnp.int32(-1) for _ in range(CAP)]
        start = [jnp.int32(steps_n) for _ in range(CAP)]
        for k in range(leaving):
            match = mig_dest[k] == d
            for c in range(CAP):
                take = match & (count == c)
                who[c] = jnp.where(take, mig_req[k], who[c])
                start[c] = jnp.where(take, resume[k], start[c])
            count = count + match.astype(jnp.int32)
        chosen = jnp.full(shape, -1, jnp.int32)
        first = jnp.full(shape, steps_n, jnp.int32)
        for c in range(CAP):
            chosen = jnp.where(slot_row // steps_n == c, who[c], chosen)
            first = jnp.where(slot_row // steps_n == c, start[c], first)
            for p in range(maxp):
                pages = pool[table[p, jnp.maximum(who[c], 0)]]
                slots[d * CAP + c, p] = jnp.where(who[c] >= 0, pages, jnp.zeros_like(pages))
        hit = (row_request == chosen) & (row_step == slot_step) & (slot_step >= first)
        select[d] = hit.astype(jnp.float32)
        return carry

    lax.fori_loop(0, ni, fill, 0)

    pl.semaphore_wait(barrier, ni - 1 + (z > 0).astype(jnp.int32) + (z < n - 1).astype(jnp.int32))

    def page_copy(k):
        to = lax.rem(me + k, ni)
        return pltpu.make_async_remote_copy(
            src_ref=slots.at[pl.ds(to * CAP, CAP)],
            dst_ref=got_ref.at[pl.ds(me * CAP, CAP)],
            send_sem=page_send.at[k],
            recv_sem=page_recv.at[k],
            device_id={"inst": to},
            device_id_type=MESH,
        )

    own_pages = pltpu.make_async_copy(
        slots.at[pl.ds(me * CAP, CAP)], got_ref.at[pl.ds(me * CAP, CAP)], own_sem.at[0]
    )
    total = jnp.zeros((h_buf.shape[1], columns), jnp.float32)
    for k in range(cuts):
        h_copy(k).wait()
        wq_copy(k).wait()
        total = total + jnp.dot(h_buf[k], wq_buf[k], preferred_element_type=jnp.float32)
    for g in range(groups):
        head = total[:, g * hd:(g + 1) * hd]
        head = head * cos_ref[...] + pltpu.roll(head, hd // 2, 1) * sin_ref[...]
        for s in range(steps_n):
            query[:, s * groups + g, :] = head[s * requests:(s + 1) * requests]

    fresh[...] = jnp.zeros_like(fresh)
    for u in range(steps_n):
        for kind in range(2):
            fresh[kind, :, u, :] = fresh_ref[
                u * requests:(u + 1) * requests, kind * hd:(kind + 1) * hd
            ].astype(jnp.float32)

    batch = 8
    old = maxp * page
    span = old + page
    column = lax.broadcasted_iota(jnp.int32, (batch * pairs, span), 1)
    step = (lax.broadcasted_iota(jnp.int32, (batch * pairs, span), 0) % pairs) // groups
    newer = (column >= old) & (column - old <= step)
    scale = hd ** (-0.5)
    empty = jnp.zeros((page - fresh.shape[2], hd), jnp.bfloat16)

    def stacked(r, kind):
        return jnp.concatenate(
            [pool[table[p, r], kind] for p in range(maxp)]
            + [fresh[kind, r].astype(jnp.bfloat16), empty],
            axis=0,
        )

    def several(i, carry):
        first = i * batch
        scores = jnp.concatenate(
            [
                lax.dot_general(
                    query[first + k].astype(jnp.bfloat16), stacked(first + k, 0),
                    (((1,), (1,)), ((), ())), preferred_element_type=jnp.float32,
                )
                for k in range(batch)
            ],
            axis=0,
        ) * scale
        length = jnp.concatenate(
            [jnp.full((pairs, span), lengths[first + k], jnp.int32) for k in range(batch)], axis=0
        )
        scores = jnp.where(newer | (column < length), scores, -1e30)
        weight = jnp.exp(scores - jnp.max(scores, axis=1, keepdims=True))
        probs = (weight / jnp.sum(weight, axis=1, keepdims=True)).astype(jnp.bfloat16)
        for k in range(batch):
            result[first + k] = jnp.dot(
                probs[k * pairs:(k + 1) * pairs], stacked(first + k, 1),
                preferred_element_type=jnp.float32,
            )
        return carry

    def up_copy(j):
        return pltpu.make_async_remote_copy(
            src_ref=up_out.at[j], dst_ref=up_in.at[j],
            send_sem=up_send.at[j], recv_sem=up_recv.at[j],
            device_id={"tp": jnp.minimum(z + 1, n - 1)}, device_id_type=MESH,
        )

    def down_copy(j):
        return pltpu.make_async_remote_copy(
            src_ref=down_out.at[j], dst_ref=down_in.at[j],
            send_sem=down_send.at[j], recv_sem=down_recv.at[j],
            device_id={"tp": jnp.maximum(z - 1, 0)}, device_id_type=MESH,
        )

    for h in range(HALVES):
        lax.fori_loop(h * some // batch, (h + 1) * some // batch, several, 0)
        for s in range(steps_n):
            for g in range(groups):
                att[h, s * some:(s + 1) * some, g * hd:(g + 1) * hd] = result[
                    h * some:(h + 1) * some, s * groups + g, :
                ].astype(jnp.bfloat16)

        def compute(k, carry, h=h):
            if h == 0:
                wo_copy(k).wait()
            value = jnp.dot(att[h], wo_buf[k], preferred_element_type=jnp.float32)
            part[h, block_of(k) * chunks + k % chunks] = value

            @pl.when((z == 0) & (k < hops))
            def _():
                up_out[h * hops + k] = value.astype(jnp.bfloat16)
                up_copy(h * hops + k).start()

            @pl.when((z == n - 1) & (k < hops))
            def _():
                down_out[h * hops + k] = value.astype(jnp.bfloat16)
                down_copy(h * hops + k).start()

            return carry

        lax.fori_loop(0, n * chunks, compute, 0)
        if h == 0:
            for k in range(1, ni):
                page_copy(k).start()
            own_pages.start()

    up_lag = jnp.maximum(z - 1, 0)
    down_lag = jnp.maximum(n - 2 - z, 0)
    for h in range(HALVES):

        def relay(j, carry, h=h):
            ju = j - up_lag
            jd = j - down_lag

            @pl.when((z > 0) & (ju >= 0) & (ju < (n - z) * chunks))
            def _():
                up_copy(h * hops + ju).wait_recv()
                spot = (n - 1 - ju // chunks) * chunks + ju % chunks
                value = part[h, spot] + up_in[h * hops + ju].astype(jnp.float32)

                @pl.when(ju < (n - 1 - z) * chunks)
                def _():
                    up_out[h * hops + ju] = value.astype(jnp.bfloat16)
                    up_copy(h * hops + ju).start()

                @pl.when(ju >= (n - 1 - z) * chunks)
                def _():
                    part[h, spot] = value

            @pl.when((z < n - 1) & (jd >= 0) & (jd < (z + 1) * chunks))
            def _():
                down_copy(h * hops + jd).wait_recv()
                value = part[h, jd] + down_in[h * hops + jd].astype(jnp.float32)

                @pl.when(jd < z * chunks)
                def _():
                    down_out[h * hops + jd] = value.astype(jnp.bfloat16)
                    down_copy(h * hops + jd).start()

                @pl.when(jd >= z * chunks)
                def _():
                    part[h, jd] = value

            return carry

        lax.fori_loop(0, hops + n - 2, relay, 0)

    selection = select[...].reshape(ni * slot_rows, HALVES * rows).astype(jnp.bfloat16)
    lane_row = lax.broadcasted_iota(jnp.int32, (rows, hd), 0)
    half = chunks // 2
    stays = []
    for h in range(HALVES):
        kept = jnp.ones((rows, hd), jnp.int32)
        for k in range(leaving):
            gone = (lane_row % some + h * some == mig_req[k]) & (lane_row // some >= resume[k])
            kept = jnp.where(gone, 0, kept)
        stays.append(jnp.concatenate([kept] * (width // hd), axis=1))
    for c in range(half):
        pieces = []
        for d in (c, c + half):
            mines = []
            for h in range(HALVES):
                mine = part[h, z * chunks + d].astype(jnp.bfloat16)
                mines.append(mine)
                kept = jnp.where(stays[h] > 0, mine.astype(jnp.float32), 0.0).astype(jnp.bfloat16)
                for s in range(steps_n):
                    home_ref[
                        s * requests + h * some:s * requests + (h + 1) * some,
                        d * width:(d + 1) * width,
                    ] = kept[s * some:(s + 1) * some]
            moved = jnp.dot(
                selection, jnp.concatenate(mines, axis=0), preferred_element_type=jnp.float32
            )
            pieces.append(moved.reshape(ni, slot_rows, width))
        leave[:, :, c * width:(c + 1) * width] = jnp.concatenate(pieces, axis=1).astype(jnp.bfloat16)

    def row_copy(k):
        to = lax.rem(me + k, ni)
        return pltpu.make_async_remote_copy(
            src_ref=leave.at[to],
            dst_ref=landed.at[me],
            send_sem=row_send.at[k],
            recv_sem=row_recv.at[k],
            device_id={"inst": to},
            device_id_type=MESH,
        )

    own_rows = pltpu.make_async_copy(leave.at[me], landed.at[me], own_sem.at[1])
    for k in range(1, ni):
        row_copy(k).start()
    own_rows.start()

    for h in range(HALVES):

        def drain(j, carry, h=h):
            @pl.when((z < n - 1) & (j < (n - 1 - z) * chunks))
            def _():
                up_copy(h * hops + j).wait_send()

            @pl.when((z > 0) & (j < z * chunks))
            def _():
                down_copy(h * hops + j).wait_send()

            return carry

        lax.fori_loop(0, hops, drain, 0)
    for k in range(1, ni):
        row_copy(k).wait()
    own_rows.wait()
    arrivals = landed[...].reshape(2 * ni * slot_rows, landed.shape[2])
    shape = (ni * slot_rows, 2 * ni * slot_rows)
    out_row = lax.broadcasted_iota(jnp.int32, shape, 0)
    in_row = lax.broadcasted_iota(jnp.int32, shape, 1)
    out_slot = out_row % (ni * CAP)
    place = (out_slot // CAP) * 2 * slot_rows + (out_slot % CAP) * steps_n + out_row // (ni * CAP)
    side = landed.shape[2]
    for d in range(2):
        order = (in_row == place + d * slot_rows).astype(jnp.float32).astype(jnp.bfloat16)
        arrive_ref[:, d * side:(d + 1) * side] = jnp.dot(
            order, arrivals, preferred_element_type=jnp.float32
        ).astype(jnp.bfloat16)
    for k in range(1, ni):
        page_copy(k).wait()
    own_pages.wait()


def local(
    hidden,
    query_weight,
    output_weight,
    kv_pool,
    new_kv,
    lengths,
    page_table,
    mig_req,
    mig_dest,
    resume,
):
    steps_n, requests, width = hidden.shape
    n = lax.axis_size("tp")
    ni = lax.axis_size("inst")
    columns = query_weight.shape[1]
    pairs = steps_n * (columns // HD)
    maxp = page_table.shape[1]
    all_rows = steps_n * requests
    rows = all_rows // HALVES
    share = output_weight.shape[1] // n
    chunk = min(1024, share // 2)
    chunks = share // chunk
    hops = (n - 1) * chunks
    slot_rows = CAP * steps_n
    position = lengths[None, :] + jnp.arange(steps_n, dtype=jnp.int32)[:, None]
    cosine, sine = turns(position.reshape(-1), HD)
    fresh = new_kv.reshape(all_rows, 2 * HD)
    cuts = 8
    vmem = pl.BlockSpec(memory_space=pltpu.VMEM)
    smem = pl.BlockSpec(memory_space=pltpu.SMEM)
    hbm = pl.BlockSpec(memory_space=pl.ANY)
    relay = pltpu.VMEM((HALVES * hops, rows, chunk), jnp.bfloat16)
    dma = pltpu.SemaphoreType.DMA
    bf16, f32 = jnp.bfloat16, jnp.float32
    slot_shape = (ni * CAP, maxp) + kv_pool.shape[1:]
    home, arrive, got_pages = pl.pallas_call(
        functools.partial(layer_kernel, n, ni, chunks),
        out_shape=(
            jax.ShapeDtypeStruct((all_rows, share), bf16),
            jax.ShapeDtypeStruct((ni * slot_rows, share), bf16),
            jax.ShapeDtypeStruct(slot_shape, bf16),
        ),
        in_specs=[smem] * 5 + [hbm] * 4 + [vmem] * 3,
        out_specs=(vmem, vmem, hbm),
        scratch_shapes=[
            pltpu.VMEM((cuts, all_rows, width // cuts), bf16),
            pltpu.VMEM((cuts, width // cuts, columns), bf16),
            pltpu.VMEM(kv_pool.shape, bf16),
            pltpu.VMEM((n * chunks, columns, chunk), bf16),
            pltpu.VMEM((requests, pairs, HD), f32),
            pltpu.VMEM((requests, pairs, HD), f32),
            pltpu.VMEM((HALVES, rows, columns), bf16),
            pltpu.VMEM((HALVES, n * chunks, rows, chunk), f32),
            relay, relay, relay, relay,
            pltpu.VMEM(slot_shape, bf16),
            pltpu.VMEM((ni, slot_rows, all_rows), f32),
            pltpu.VMEM((ni, 2 * slot_rows, share // 2), bf16),
            pltpu.VMEM((ni, 2 * slot_rows, share // 2), bf16),
            pltpu.VMEM((2, requests, 16, HD), f32),
            dma((cuts,)), dma((cuts,)), dma, dma((n * chunks,)),
            dma((HALVES * hops,)), dma((HALVES * hops,)), dma((HALVES * hops,)), dma((HALVES * hops,)),
            dma((ni,)), dma((ni,)), dma((ni,)), dma((ni,)), dma((2,)),
        ],
        compiler_params=pltpu.CompilerParams(
            collective_id=0, has_side_effects=True, vmem_limit_bytes=60 * 1024 * 1024
        ),
    )(
        lengths, page_table.T, mig_req, mig_dest.reshape(-1), resume,
        hidden.reshape(-1, width), query_weight, kv_pool, output_weight, fresh, cosine, sine,
    )
    home = home.reshape(steps_n, requests, -1)
    arrival = arrive.reshape(steps_n, ni * CAP, -1)
    return (home, arrival, got_pages)


def solution(mesh):
    in_specs = (
        P(None, "inst", None),
        P(None, "tp"),
        P("tp", None),
        P("inst", None, None, "tp"),
        P(None, "inst", None, "tp"),
        P("inst"),
        P("inst", None),
        P("inst"),
        P("inst", None),
        P("inst"),
    )
    out_specs = (P(None, "inst", "tp"), P(None, "inst", "tp"), P("inst", None, None, None, "tp"))
    return jax.shard_map(local, mesh=mesh, in_specs=in_specs, out_specs=out_specs, check_vma=False)
```

```python
import functools

import jax
import jax.numpy as jnp
from jax import lax
from jax.experimental import pallas as pl
from jax.experimental.pallas import tpu as pltpu
from jax.sharding import PartitionSpec as P

HD = 128
CAP = 2
HALVES = 2


ROPE_BASE = 500000.0

MESH = pl.DeviceIdType.MESH


def turns(position, depth):
    half = depth // 2
    index = jnp.arange(depth, dtype=jnp.int32)
    inverse = ROPE_BASE ** (-(index % half).astype(jnp.float32) * 2.0 / depth)
    angles = position.astype(jnp.float32)[:, None] * inverse
    sign = jnp.where(index < half, -1.0, 1.0).astype(jnp.float32)
    return jnp.cos(angles), jnp.sin(angles) * sign


def emit_kernel(*refs):
    count = (len(refs) - 1) // 2
    sems = refs[-1]
    copies = []
    for source, target in zip(refs[:count], refs[count:2 * count]):
        for k in range(source.shape[0]):
            copies.append(
                pltpu.make_async_copy(source.at[k], target.at[k], sems.at[len(copies)])
            )
    for copy in copies:
        copy.start()
    for copy in copies:
        copy.wait()


def emit(*arrays):
    hbm = pl.BlockSpec(memory_space=pl.ANY)
    return pl.pallas_call(
        emit_kernel,
        out_shape=tuple(jax.ShapeDtypeStruct(x.shape, x.dtype) for x in arrays),
        in_specs=[hbm] * len(arrays),
        out_specs=(hbm,) * len(arrays),
        scratch_shapes=[pltpu.SemaphoreType.DMA((sum(x.shape[0] for x in arrays),))],
        compiler_params=pltpu.CompilerParams(vmem_limit_bytes=60 * 1024 * 1024),
    )(*arrays)


def layer_kernel(
    n, ni, chunks,
    lengths, table, mig_req, mig_dest, resume,
    hidden_ref, wq_ref, pool_ref, wo_ref, fresh_ref, cos_ref, sin_ref,
    home_ref, arrive_ref, got_ref,
    h_buf, wq_buf, pool, wo_buf, query, result, att, part, up_in, down_in, up_out, down_out,
    slots, select, leave, landed, fresh,
    h_sem, wq_sem, pool_sem, wo_sem,
    up_send, up_recv, down_send, down_recv, page_send, page_recv, row_send, row_recv, own_sem,
):
    z = lax.axis_index("tp")
    me = lax.axis_index("inst")
    cuts, depth, columns = wq_buf.shape
    requests, pairs, hd = query.shape
    groups = columns // hd
    steps_n = pairs // groups
    page = pool.shape[2]
    maxp = table.shape[0]
    leaving = mig_req.shape[0]
    some = requests // HALVES
    rows, width = part.shape[2:]
    hops = (n - 1) * chunks
    low = z < n // 2

    def h_copy(k):
        return pltpu.make_async_copy(
            hidden_ref.at[:, pl.ds(k * depth, depth)], h_buf.at[k], h_sem.at[k]
        )

    def wq_copy(k):
        return pltpu.make_async_copy(
            wq_ref.at[pl.ds(k * depth, depth)], wq_buf.at[k], wq_sem.at[k]
        )

    def block_of(k):
        return jnp.where(low, n - 1 - k // chunks, k // chunks)

    def wo_copy(k):
        column = (block_of(k) * chunks + k % chunks) * width
        return pltpu.make_async_copy(
            wo_ref.at[:, pl.ds(pl.multiple_of(column, width), width)], wo_buf.at[k], wo_sem.at[k]
        )

    pool_copy = pltpu.make_async_copy(pool_ref, pool, pool_sem)
    for k in range(cuts):
        h_copy(k).start()
        wq_copy(k).start()
    pool_copy.start()

    barrier = pltpu.get_barrier_semaphore()
    for k in range(1, ni):
        pl.semaphore_signal(
            barrier, inc=1, device_id={"inst": lax.rem(me + k, ni)}, device_id_type=MESH
        )

    @pl.when(z > 0)
    def _():
        pl.semaphore_signal(barrier, inc=1, device_id={"tp": z - 1}, device_id_type=MESH)

    @pl.when(z < n - 1)
    def _():
        pl.semaphore_signal(barrier, inc=1, device_id={"tp": z + 1}, device_id_type=MESH)

    slot_rows = CAP * steps_n
    shape = (slot_rows, HALVES * rows)
    slot_row = lax.broadcasted_iota(jnp.int32, shape, 0)
    row = lax.broadcasted_iota(jnp.int32, shape, 1)
    slot_step = slot_row % steps_n
    row_request = (row // rows) * some + row % some
    row_step = (row % rows) // some

    def fill(d, carry):
        count = jnp.int32(0)
        who = [jnp.int32(-1) for _ in range(CAP)]
        start = [jnp.int32(steps_n) for _ in range(CAP)]
        for k in range(leaving):
            match = mig_dest[k] == d
            for c in range(CAP):
                take = match & (count == c)
                who[c] = jnp.where(take, mig_req[k], who[c])
                start[c] = jnp.where(take, resume[k], start[c])
            count = count + match.astype(jnp.int32)
        chosen = jnp.full(shape, -1, jnp.int32)
        first = jnp.full(shape, steps_n, jnp.int32)
        for c in range(CAP):
            chosen = jnp.where(slot_row // steps_n == c, who[c], chosen)
            first = jnp.where(slot_row // steps_n == c, start[c], first)
            for p in range(maxp):
                pages = pool[table[p, jnp.maximum(who[c], 0)]]
                slots[d * CAP + c, p] = jnp.where(who[c] >= 0, pages, jnp.zeros_like(pages))
        hit = (row_request == chosen) & (row_step == slot_step) & (slot_step >= first)
        select[d] = hit.astype(jnp.float32)
        return carry

    def page_copy(k):
        to = lax.rem(me + k, ni)
        return pltpu.make_async_remote_copy(
            src_ref=slots.at[pl.ds(to * CAP, CAP)],
            dst_ref=got_ref.at[pl.ds(me * CAP, CAP)],
            send_sem=page_send.at[k],
            recv_sem=page_recv.at[k],
            device_id={"inst": to},
            device_id_type=MESH,
        )

    own_pages = pltpu.make_async_copy(
        slots.at[pl.ds(me * CAP, CAP)], got_ref.at[pl.ds(me * CAP, CAP)], own_sem.at[0]
    )
    total = jnp.zeros((h_buf.shape[1], columns), jnp.float32)
    for k in range(cuts):
        h_copy(k).wait()
        wq_copy(k).wait()
        if k == cuts - 2:
            for c in range(n * chunks):
                wo_copy(c).start()
        total = total + jnp.dot(h_buf[k], wq_buf[k], preferred_element_type=jnp.float32)
    for g in range(groups):
        head = total[:, g * hd:(g + 1) * hd]
        head = head * cos_ref[...] + pltpu.roll(head, hd // 2, 1) * sin_ref[...]
        for s in range(steps_n):
            query[:, s * groups + g, :] = head[s * requests:(s + 1) * requests]

    pl.semaphore_wait(barrier, ni - 1 + (z > 0).astype(jnp.int32) + (z < n - 1).astype(jnp.int32))

    fresh[...] = jnp.zeros_like(fresh)
    for u in range(steps_n):
        for kind in range(2):
            fresh[kind, :, u, :] = fresh_ref[
                u * requests:(u + 1) * requests, kind * hd:(kind + 1) * hd
            ].astype(jnp.float32)

    pool_copy.wait()
    batch = 8
    old = maxp * page
    span = old + page
    column = lax.broadcasted_iota(jnp.int32, (batch * pairs, span), 1)
    step = (lax.broadcasted_iota(jnp.int32, (batch * pairs, span), 0) % pairs) // groups
    newer = (column >= old) & (column - old <= step)
    scale = hd ** (-0.5)
    empty = jnp.zeros((page - fresh.shape[2], hd), jnp.bfloat16)

    def stacked(r, kind):
        return jnp.concatenate(
            [pool[table[p, r], kind] for p in range(maxp)]
            + [fresh[kind, r].astype(jnp.bfloat16), empty],
            axis=0,
        )

    def several(i, carry):
        first = i * batch
        scores = jnp.concatenate(
            [
                lax.dot_general(
                    query[first + k].astype(jnp.bfloat16), stacked(first + k, 0),
                    (((1,), (1,)), ((), ())), preferred_element_type=jnp.float32,
                )
                for k in range(batch)
            ],
            axis=0,
        ) * scale
        length = jnp.concatenate(
            [jnp.full((pairs, span), lengths[first + k], jnp.int32) for k in range(batch)], axis=0
        )
        scores = jnp.where(newer | (column < length), scores, -1e30)
        weight = jnp.exp(scores - jnp.max(scores, axis=1, keepdims=True))
        probs = (weight / jnp.sum(weight, axis=1, keepdims=True)).astype(jnp.bfloat16)
        for k in range(batch):
            result[first + k] = jnp.dot(
                probs[k * pairs:(k + 1) * pairs], stacked(first + k, 1),
                preferred_element_type=jnp.float32,
            )
        return carry

    def up_copy(j):
        return pltpu.make_async_remote_copy(
            src_ref=up_out.at[j], dst_ref=up_in.at[j],
            send_sem=up_send.at[j], recv_sem=up_recv.at[j],
            device_id={"tp": jnp.minimum(z + 1, n - 1)}, device_id_type=MESH,
        )

    def down_copy(j):
        return pltpu.make_async_remote_copy(
            src_ref=down_out.at[j], dst_ref=down_in.at[j],
            send_sem=down_send.at[j], recv_sem=down_recv.at[j],
            device_id={"tp": jnp.maximum(z - 1, 0)}, device_id_type=MESH,
        )

    for h in range(HALVES):
        lax.fori_loop(h * some // batch, (h + 1) * some // batch, several, 0)
        for s in range(steps_n):
            for g in range(groups):
                att[h, s * some:(s + 1) * some, g * hd:(g + 1) * hd] = result[
                    h * some:(h + 1) * some, s * groups + g, :
                ].astype(jnp.bfloat16)

        def compute(k, carry, h=h):
            if h == 0:
                wo_copy(k).wait()
            value = jnp.dot(att[h], wo_buf[k], preferred_element_type=jnp.float32)
            part[h, block_of(k) * chunks + k % chunks] = value

            @pl.when((z == 0) & (k < hops))
            def _():
                up_out[h * hops + k] = value.astype(jnp.bfloat16)
                up_copy(h * hops + k).start()

            @pl.when((z == n - 1) & (k < hops))
            def _():
                down_out[h * hops + k] = value.astype(jnp.bfloat16)
                down_copy(h * hops + k).start()

            return carry

        lax.fori_loop(0, n * chunks, compute, 0)
        if h == 0:
            lax.fori_loop(0, ni, fill, 0)
            for k in range(1, ni):
                page_copy(k).start()
            own_pages.start()

    up_lag = jnp.maximum(z - 1, 0)
    down_lag = jnp.maximum(n - 2 - z, 0)
    for h in range(HALVES):

        def relay(j, carry, h=h):
            ju = j - up_lag
            jd = j - down_lag

            @pl.when((z > 0) & (ju >= 0) & (ju < (n - z) * chunks))
            def _():
                up_copy(h * hops + ju).wait_recv()
                spot = (n - 1 - ju // chunks) * chunks + ju % chunks
                value = part[h, spot] + up_in[h * hops + ju].astype(jnp.float32)

                @pl.when(ju < (n - 1 - z) * chunks)
                def _():
                    up_out[h * hops + ju] = value.astype(jnp.bfloat16)
                    up_copy(h * hops + ju).start()

                @pl.when(ju >= (n - 1 - z) * chunks)
                def _():
                    part[h, spot] = value

            @pl.when((z < n - 1) & (jd >= 0) & (jd < (z + 1) * chunks))
            def _():
                down_copy(h * hops + jd).wait_recv()
                value = part[h, jd] + down_in[h * hops + jd].astype(jnp.float32)

                @pl.when(jd < z * chunks)
                def _():
                    down_out[h * hops + jd] = value.astype(jnp.bfloat16)
                    down_copy(h * hops + jd).start()

                @pl.when(jd >= z * chunks)
                def _():
                    part[h, jd] = value

            return carry

        lax.fori_loop(0, hops + n - 2, relay, 0)

    selection = select[...].reshape(ni * slot_rows, HALVES * rows).astype(jnp.bfloat16)
    lane_row = lax.broadcasted_iota(jnp.int32, (rows, hd), 0)
    half = chunks // 2
    stays = []
    for h in range(HALVES):
        kept = jnp.ones((rows, hd), jnp.int32)
        for k in range(leaving):
            gone = (lane_row % some + h * some == mig_req[k]) & (lane_row // some >= resume[k])
            kept = jnp.where(gone, 0, kept)
        stays.append(jnp.concatenate([kept] * (width // hd), axis=1))
    for c in range(half):
        pieces = []
        for d in (c, c + half):
            mines = []
            for h in range(HALVES):
                mine = part[h, z * chunks + d].astype(jnp.bfloat16)
                mines.append(mine)
                kept = jnp.where(stays[h] > 0, mine.astype(jnp.float32), 0.0).astype(jnp.bfloat16)
                for s in range(steps_n):
                    home_ref[
                        s * requests + h * some:s * requests + (h + 1) * some,
                        d * width:(d + 1) * width,
                    ] = kept[s * some:(s + 1) * some]
            moved = jnp.dot(
                selection, jnp.concatenate(mines, axis=0), preferred_element_type=jnp.float32
            )
            pieces.append(moved.reshape(ni, slot_rows, width))
        leave[:, :, c * width:(c + 1) * width] = jnp.concatenate(pieces, axis=1).astype(jnp.bfloat16)

    def row_copy(k):
        to = lax.rem(me + k, ni)
        return pltpu.make_async_remote_copy(
            src_ref=leave.at[to],
            dst_ref=landed.at[me],
            send_sem=row_send.at[k],
            recv_sem=row_recv.at[k],
            device_id={"inst": to},
            device_id_type=MESH,
        )

    own_rows = pltpu.make_async_copy(leave.at[me], landed.at[me], own_sem.at[1])
    for k in range(1, ni):
        row_copy(k).start()
    own_rows.start()

    for h in range(HALVES):

        def drain(j, carry, h=h):
            @pl.when((z < n - 1) & (j < (n - 1 - z) * chunks))
            def _():
                up_copy(h * hops + j).wait_send()

            @pl.when((z > 0) & (j < z * chunks))
            def _():
                down_copy(h * hops + j).wait_send()

            return carry

        lax.fori_loop(0, hops, drain, 0)
    for k in range(1, ni):
        row_copy(k).wait()
    own_rows.wait()
    arrivals = landed[...].reshape(2 * ni * slot_rows, landed.shape[2])
    shape = (ni * slot_rows, 2 * ni * slot_rows)
    out_row = lax.broadcasted_iota(jnp.int32, shape, 0)
    in_row = lax.broadcasted_iota(jnp.int32, shape, 1)
    out_slot = out_row % (ni * CAP)
    place = (out_slot // CAP) * 2 * slot_rows + (out_slot % CAP) * steps_n + out_row // (ni * CAP)
    side = landed.shape[2]
    for d in range(2):
        order = (in_row == place + d * slot_rows).astype(jnp.float32).astype(jnp.bfloat16)
        arrive_ref[:, d * side:(d + 1) * side] = jnp.dot(
            order, arrivals, preferred_element_type=jnp.float32
        ).astype(jnp.bfloat16)
    for k in range(1, ni):
        page_copy(k).wait()
    own_pages.wait()


def local(
    hidden,
    query_weight,
    output_weight,
    kv_pool,
    new_kv,
    lengths,
    page_table,
    mig_req,
    mig_dest,
    resume,
):
    steps_n, requests, width = hidden.shape
    n = lax.axis_size("tp")
    ni = lax.axis_size("inst")
    columns = query_weight.shape[1]
    pairs = steps_n * (columns // HD)
    maxp = page_table.shape[1]
    all_rows = steps_n * requests
    rows = all_rows // HALVES
    share = output_weight.shape[1] // n
    chunk = min(1024, share // 2)
    chunks = share // chunk
    hops = (n - 1) * chunks
    slot_rows = CAP * steps_n
    position = lengths[None, :] + jnp.arange(steps_n, dtype=jnp.int32)[:, None]
    cosine, sine = turns(position.reshape(-1), HD)
    fresh = new_kv.reshape(all_rows, 2 * HD)
    cuts = 8
    vmem = pl.BlockSpec(memory_space=pltpu.VMEM)
    smem = pl.BlockSpec(memory_space=pltpu.SMEM)
    hbm = pl.BlockSpec(memory_space=pl.ANY)
    relay = pltpu.VMEM((HALVES * hops, rows, chunk), jnp.bfloat16)
    dma = pltpu.SemaphoreType.DMA
    bf16, f32 = jnp.bfloat16, jnp.float32
    slot_shape = (ni * CAP, maxp) + kv_pool.shape[1:]
    home, arrive, got_pages = pl.pallas_call(
        functools.partial(layer_kernel, n, ni, chunks),
        out_shape=(
            jax.ShapeDtypeStruct((all_rows, share), bf16),
            jax.ShapeDtypeStruct((ni * slot_rows, share), bf16),
            jax.ShapeDtypeStruct(slot_shape, bf16),
        ),
        in_specs=[smem] * 5 + [hbm] * 4 + [vmem] * 3,
        out_specs=(vmem, vmem, hbm),
        scratch_shapes=[
            pltpu.VMEM((cuts, all_rows, width // cuts), bf16),
            pltpu.VMEM((cuts, width // cuts, columns), bf16),
            pltpu.VMEM(kv_pool.shape, bf16),
            pltpu.VMEM((n * chunks, columns, chunk), bf16),
            pltpu.VMEM((requests, pairs, HD), f32),
            pltpu.VMEM((requests, pairs, HD), f32),
            pltpu.VMEM((HALVES, rows, columns), bf16),
            pltpu.VMEM((HALVES, n * chunks, rows, chunk), f32),
            relay, relay, relay, relay,
            pltpu.VMEM(slot_shape, bf16),
            pltpu.VMEM((ni, slot_rows, all_rows), f32),
            pltpu.VMEM((ni, 2 * slot_rows, share // 2), bf16),
            pltpu.VMEM((ni, 2 * slot_rows, share // 2), bf16),
            pltpu.VMEM((2, requests, 16, HD), f32),
            dma((cuts,)), dma((cuts,)), dma, dma((n * chunks,)),
            dma((HALVES * hops,)), dma((HALVES * hops,)), dma((HALVES * hops,)), dma((HALVES * hops,)),
            dma((ni,)), dma((ni,)), dma((ni,)), dma((ni,)), dma((2,)),
        ],
        compiler_params=pltpu.CompilerParams(
            collective_id=0, has_side_effects=True, vmem_limit_bytes=60 * 1024 * 1024
        ),
    )(
        lengths, page_table.T, mig_req, mig_dest.reshape(-1), resume,
        hidden.reshape(-1, width), query_weight, kv_pool, output_weight, fresh, cosine, sine,
    )
    home = home.reshape(steps_n, requests, -1)
    arrival = arrive.reshape(steps_n, ni * CAP, -1)
    return emit(home, arrival, got_pages)


def solution(mesh):
    in_specs = (
        P(None, "inst", None),
        P(None, "tp"),
        P("tp", None),
        P("inst", None, None, "tp"),
        P(None, "inst", None, "tp"),
        P("inst"),
        P("inst", None),
        P("inst"),
        P("inst", None),
        P("inst"),
    )
    out_specs = (P(None, "inst", "tp"), P(None, "inst", "tp"), P("inst", None, None, None, "tp"))
    return jax.shard_map(local, mesh=mesh, in_specs=in_specs, out_specs=out_specs, check_vma=False)
```

```python
import functools

import jax
import jax.numpy as jnp
from jax import lax
from jax.experimental import pallas as pl
from jax.experimental.pallas import tpu as pltpu
from jax.sharding import PartitionSpec as P

HD = 128
CAP = 2
HALVES = 2


ROPE_BASE = 500000.0

MESH = pl.DeviceIdType.MESH


def turns(position, depth):
    half = depth // 2
    index = jnp.arange(depth, dtype=jnp.int32)
    inverse = ROPE_BASE ** (-(index % half).astype(jnp.float32) * 2.0 / depth)
    angles = position.astype(jnp.float32)[:, None] * inverse
    sign = jnp.where(index < half, -1.0, 1.0).astype(jnp.float32)
    return jnp.cos(angles), jnp.sin(angles) * sign


def emit_kernel(count, *refs):
    sources, targets = refs[:count], refs[count:2 * count]
    buffers = refs[2 * count:3 * count]
    in_sems, out_sems = refs[3 * count:]
    ins, outs = [], []
    for source, buffer, target in zip(sources, buffers, targets):
        for k in range(source.shape[0]):
            ins.append(pltpu.make_async_copy(source.at[k], buffer.at[k], in_sems.at[len(ins)]))
            outs.append(pltpu.make_async_copy(buffer.at[k], target.at[k], out_sems.at[len(outs)]))
    for copy in ins:
        copy.start()
    for first, second in zip(ins, outs):
        first.wait()
        second.start()
    for copy in outs:
        copy.wait()


def emit(*arrays):
    hbm = pl.BlockSpec(memory_space=pl.ANY)
    pieces = sum(x.shape[0] for x in arrays)
    return pl.pallas_call(
        functools.partial(emit_kernel, len(arrays)),
        out_shape=tuple(jax.ShapeDtypeStruct(x.shape, x.dtype) for x in arrays),
        in_specs=[hbm] * len(arrays),
        out_specs=(hbm,) * len(arrays),
        scratch_shapes=[pltpu.VMEM(x.shape, x.dtype) for x in arrays]
        + [pltpu.SemaphoreType.DMA((pieces,)), pltpu.SemaphoreType.DMA((pieces,))],
        compiler_params=pltpu.CompilerParams(vmem_limit_bytes=60 * 1024 * 1024),
    )(*arrays)


def layer_kernel(
    n, ni, chunks,
    lengths, table, mig_req, mig_dest, resume,
    hidden_ref, wq_ref, pool_ref, wo_ref, fresh_ref, cos_ref, sin_ref,
    home_ref, arrive_ref, got_ref,
    h_buf, wq_buf, pool, wo_buf, query, result, att, part, up_in, down_in, up_out, down_out,
    slots, select, leave, landed, fresh,
    h_sem, wq_sem, pool_sem, wo_sem,
    up_send, up_recv, down_send, down_recv, page_send, page_recv, row_send, row_recv, own_sem,
):
    z = lax.axis_index("tp")
    me = lax.axis_index("inst")
    cuts, depth, columns = wq_buf.shape
    requests, pairs, hd = query.shape
    groups = columns // hd
    steps_n = pairs // groups
    page = pool.shape[2]
    maxp = table.shape[0]
    leaving = mig_req.shape[0]
    some = requests // HALVES
    rows, width = part.shape[2:]
    hops = (n - 1) * chunks
    low = z < n // 2

    def h_copy(k):
        return pltpu.make_async_copy(
            hidden_ref.at[:, pl.ds(k * depth, depth)], h_buf.at[k], h_sem.at[k]
        )

    def wq_copy(k):
        return pltpu.make_async_copy(
            wq_ref.at[pl.ds(k * depth, depth)], wq_buf.at[k], wq_sem.at[k]
        )

    def block_of(k):
        return jnp.where(low, n - 1 - k // chunks, k // chunks)

    def wo_copy(k):
        column = (block_of(k) * chunks + k % chunks) * width
        return pltpu.make_async_copy(
            wo_ref.at[:, pl.ds(pl.multiple_of(column, width), width)], wo_buf.at[k], wo_sem.at[k]
        )

    pool_copy = pltpu.make_async_copy(pool_ref, pool, pool_sem)
    for k in range(cuts):
        h_copy(k).start()
        wq_copy(k).start()
    pool_copy.start()

    barrier = pltpu.get_barrier_semaphore()
    for k in range(1, ni):
        pl.semaphore_signal(
            barrier, inc=1, device_id={"inst": lax.rem(me + k, ni)}, device_id_type=MESH
        )

    @pl.when(z > 0)
    def _():
        pl.semaphore_signal(barrier, inc=1, device_id={"tp": z - 1}, device_id_type=MESH)

    @pl.when(z < n - 1)
    def _():
        pl.semaphore_signal(barrier, inc=1, device_id={"tp": z + 1}, device_id_type=MESH)

    slot_rows = CAP * steps_n
    shape = (slot_rows, HALVES * rows)
    slot_row = lax.broadcasted_iota(jnp.int32, shape, 0)
    row = lax.broadcasted_iota(jnp.int32, shape, 1)
    slot_step = slot_row % steps_n
    row_request = (row // rows) * some + row % some
    row_step = (row % rows) // some

    def fill(d, carry):
        count = jnp.int32(0)
        who = [jnp.int32(-1) for _ in range(CAP)]
        start = [jnp.int32(steps_n) for _ in range(CAP)]
        for k in range(leaving):
            match = mig_dest[k] == d
            for c in range(CAP):
                take = match & (count == c)
                who[c] = jnp.where(take, mig_req[k], who[c])
                start[c] = jnp.where(take, resume[k], start[c])
            count = count + match.astype(jnp.int32)
        chosen = jnp.full(shape, -1, jnp.int32)
        first = jnp.full(shape, steps_n, jnp.int32)
        for c in range(CAP):
            chosen = jnp.where(slot_row // steps_n == c, who[c], chosen)
            first = jnp.where(slot_row // steps_n == c, start[c], first)
            for p in range(maxp):
                pages = pool[table[p, jnp.maximum(who[c], 0)]]
                slots[d * CAP + c, p] = jnp.where(who[c] >= 0, pages, jnp.zeros_like(pages))
        hit = (row_request == chosen) & (row_step == slot_step) & (slot_step >= first)
        select[d] = hit.astype(jnp.float32)
        return carry

    def page_copy(k):
        to = lax.rem(me + k, ni)
        return pltpu.make_async_remote_copy(
            src_ref=slots.at[pl.ds(to * CAP, CAP)],
            dst_ref=got_ref.at[pl.ds(me * CAP, CAP)],
            send_sem=page_send.at[k],
            recv_sem=page_recv.at[k],
            device_id={"inst": to},
            device_id_type=MESH,
        )

    own_pages = pltpu.make_async_copy(
        slots.at[pl.ds(me * CAP, CAP)], got_ref.at[pl.ds(me * CAP, CAP)], own_sem.at[0]
    )
    total = jnp.zeros((h_buf.shape[1], columns), jnp.float32)
    for k in range(cuts):
        h_copy(k).wait()
        wq_copy(k).wait()
        if k == cuts - 2:
            for c in range(n * chunks):
                wo_copy(c).start()
        total = total + jnp.dot(h_buf[k], wq_buf[k], preferred_element_type=jnp.float32)
    for g in range(groups):
        head = total[:, g * hd:(g + 1) * hd]
        head = head * cos_ref[...] + pltpu.roll(head, hd // 2, 1) * sin_ref[...]
        for s in range(steps_n):
            query[:, s * groups + g, :] = head[s * requests:(s + 1) * requests]

    pl.semaphore_wait(barrier, ni - 1 + (z > 0).astype(jnp.int32) + (z < n - 1).astype(jnp.int32))

    fresh[...] = jnp.zeros_like(fresh)
    for u in range(steps_n):
        for kind in range(2):
            fresh[kind, :, u, :] = fresh_ref[
                u * requests:(u + 1) * requests, kind * hd:(kind + 1) * hd
            ].astype(jnp.float32)

    pool_copy.wait()
    batch = 8
    old = maxp * page
    span = old + page
    column = lax.broadcasted_iota(jnp.int32, (batch * pairs, span), 1)
    step = (lax.broadcasted_iota(jnp.int32, (batch * pairs, span), 0) % pairs) // groups
    newer = (column >= old) & (column - old <= step)
    scale = hd ** (-0.5)
    empty = jnp.zeros((page - fresh.shape[2], hd), jnp.bfloat16)

    def stacked(r, kind):
        return jnp.concatenate(
            [pool[table[p, r], kind] for p in range(maxp)]
            + [fresh[kind, r].astype(jnp.bfloat16), empty],
            axis=0,
        )

    def several(i, carry):
        first = i * batch
        scores = jnp.concatenate(
            [
                lax.dot_general(
                    query[first + k].astype(jnp.bfloat16), stacked(first + k, 0),
                    (((1,), (1,)), ((), ())), preferred_element_type=jnp.float32,
                )
                for k in range(batch)
            ],
            axis=0,
        ) * scale
        length = jnp.concatenate(
            [jnp.full((pairs, span), lengths[first + k], jnp.int32) for k in range(batch)], axis=0
        )
        scores = jnp.where(newer | (column < length), scores, -1e30)
        weight = jnp.exp(scores - jnp.max(scores, axis=1, keepdims=True))
        probs = (weight / jnp.sum(weight, axis=1, keepdims=True)).astype(jnp.bfloat16)
        for k in range(batch):
            result[first + k] = jnp.dot(
                probs[k * pairs:(k + 1) * pairs], stacked(first + k, 1),
                preferred_element_type=jnp.float32,
            )
        return carry

    def up_copy(j):
        return pltpu.make_async_remote_copy(
            src_ref=up_out.at[j], dst_ref=up_in.at[j],
            send_sem=up_send.at[j], recv_sem=up_recv.at[j],
            device_id={"tp": jnp.minimum(z + 1, n - 1)}, device_id_type=MESH,
        )

    def down_copy(j):
        return pltpu.make_async_remote_copy(
            src_ref=down_out.at[j], dst_ref=down_in.at[j],
            send_sem=down_send.at[j], recv_sem=down_recv.at[j],
            device_id={"tp": jnp.maximum(z - 1, 0)}, device_id_type=MESH,
        )

    for h in range(HALVES):
        lax.fori_loop(h * some // batch, (h + 1) * some // batch, several, 0)
        for s in range(steps_n):
            for g in range(groups):
                att[h, s * some:(s + 1) * some, g * hd:(g + 1) * hd] = result[
                    h * some:(h + 1) * some, s * groups + g, :
                ].astype(jnp.bfloat16)

        def compute(k, carry, h=h):
            if h == 0:
                wo_copy(k).wait()
            value = jnp.dot(att[h], wo_buf[k], preferred_element_type=jnp.float32)
            part[h, block_of(k) * chunks + k % chunks] = value

            @pl.when((z == 0) & (k < hops))
            def _():
                up_out[h * hops + k] = value.astype(jnp.bfloat16)
                up_copy(h * hops + k).start()

            @pl.when((z == n - 1) & (k < hops))
            def _():
                down_out[h * hops + k] = value.astype(jnp.bfloat16)
                down_copy(h * hops + k).start()

            return carry

        lax.fori_loop(0, n * chunks, compute, 0)
        if h == 0:
            lax.fori_loop(0, ni, fill, 0)
            for k in range(1, ni):
                page_copy(k).start()
            own_pages.start()

    selection = select[...].reshape(ni * slot_rows, HALVES * rows).astype(jnp.bfloat16)
    lane_row = lax.broadcasted_iota(jnp.int32, (rows, hd), 0)
    half = chunks // 2
    stays = []
    for h in range(HALVES):
        kept = jnp.ones((rows, hd), jnp.int32)
        for k in range(leaving):
            gone = (lane_row % some + h * some == mig_req[k]) & (lane_row // some >= resume[k])
            kept = jnp.where(gone, 0, kept)
        stays.append(jnp.concatenate([kept] * (width // hd), axis=1))
    up_lag = jnp.maximum(z - 1, 0)
    down_lag = jnp.maximum(n - 2 - z, 0)
    for h in range(HALVES):

        def relay(j, carry, h=h):
            ju = j - up_lag
            jd = j - down_lag

            @pl.when((z > 0) & (ju >= 0) & (ju < (n - z) * chunks))
            def _():
                up_copy(h * hops + ju).wait_recv()
                spot = (n - 1 - ju // chunks) * chunks + ju % chunks
                value = part[h, spot] + up_in[h * hops + ju].astype(jnp.float32)

                @pl.when(ju < (n - 1 - z) * chunks)
                def _():
                    up_out[h * hops + ju] = value.astype(jnp.bfloat16)
                    up_copy(h * hops + ju).start()

                @pl.when(ju >= (n - 1 - z) * chunks)
                def _():
                    part[h, spot] = value

            @pl.when((z < n - 1) & (jd >= 0) & (jd < (z + 1) * chunks))
            def _():
                down_copy(h * hops + jd).wait_recv()
                value = part[h, jd] + down_in[h * hops + jd].astype(jnp.float32)

                @pl.when(jd < z * chunks)
                def _():
                    down_out[h * hops + jd] = value.astype(jnp.bfloat16)
                    down_copy(h * hops + jd).start()

                @pl.when(jd >= z * chunks)
                def _():
                    part[h, jd] = value

            return carry

        lax.fori_loop(0, hops + n - 2, relay, 0)

    for c in range(half):
        pieces = []
        for d in (c, c + half):
            mines = []
            for h in range(HALVES):
                mine = part[h, z * chunks + d].astype(jnp.bfloat16)
                mines.append(mine)
                kept = jnp.where(stays[h] > 0, mine.astype(jnp.float32), 0.0).astype(jnp.bfloat16)
                for s in range(steps_n):
                    home_ref[
                        s * requests + h * some:s * requests + (h + 1) * some,
                        d * width:(d + 1) * width,
                    ] = kept[s * some:(s + 1) * some]
            moved = jnp.dot(
                selection, jnp.concatenate(mines, axis=0), preferred_element_type=jnp.float32
            )
            pieces.append(moved.reshape(ni, slot_rows, width))
        leave[:, :, c * width:(c + 1) * width] = jnp.concatenate(pieces, axis=1).astype(jnp.bfloat16)

    def row_copy(k):
        to = lax.rem(me + k, ni)
        return pltpu.make_async_remote_copy(
            src_ref=leave.at[to],
            dst_ref=landed.at[me],
            send_sem=row_send.at[k],
            recv_sem=row_recv.at[k],
            device_id={"inst": to},
            device_id_type=MESH,
        )

    own_rows = pltpu.make_async_copy(leave.at[me], landed.at[me], own_sem.at[1])
    for k in range(1, ni):
        row_copy(k).start()
    own_rows.start()

    for h in range(HALVES):

        def drain(j, carry, h=h):
            @pl.when((z < n - 1) & (j < (n - 1 - z) * chunks))
            def _():
                up_copy(h * hops + j).wait_send()

            @pl.when((z > 0) & (j < z * chunks))
            def _():
                down_copy(h * hops + j).wait_send()

            return carry

        lax.fori_loop(0, hops, drain, 0)
    for k in range(1, ni):
        row_copy(k).wait()
    own_rows.wait()
    arrivals = landed[...].reshape(2 * ni * slot_rows, landed.shape[2])
    shape = (ni * slot_rows, 2 * ni * slot_rows)
    out_row = lax.broadcasted_iota(jnp.int32, shape, 0)
    in_row = lax.broadcasted_iota(jnp.int32, shape, 1)
    out_slot = out_row % (ni * CAP)
    place = (out_slot // CAP) * 2 * slot_rows + (out_slot % CAP) * steps_n + out_row // (ni * CAP)
    side = landed.shape[2]
    for d in range(2):
        order = (in_row == place + d * slot_rows).astype(jnp.float32).astype(jnp.bfloat16)
        arrive_ref[:, d * side:(d + 1) * side] = jnp.dot(
            order, arrivals, preferred_element_type=jnp.float32
        ).astype(jnp.bfloat16)
    for k in range(1, ni):
        page_copy(k).wait()
    own_pages.wait()


def local(
    hidden,
    query_weight,
    output_weight,
    kv_pool,
    new_kv,
    lengths,
    page_table,
    mig_req,
    mig_dest,
    resume,
):
    steps_n, requests, width = hidden.shape
    n = lax.axis_size("tp")
    ni = lax.axis_size("inst")
    columns = query_weight.shape[1]
    pairs = steps_n * (columns // HD)
    maxp = page_table.shape[1]
    all_rows = steps_n * requests
    rows = all_rows // HALVES
    share = output_weight.shape[1] // n
    chunk = min(1024, share // 2)
    chunks = share // chunk
    hops = (n - 1) * chunks
    slot_rows = CAP * steps_n
    position = lengths[None, :] + jnp.arange(steps_n, dtype=jnp.int32)[:, None]
    cosine, sine = turns(position.reshape(-1), HD)
    fresh = new_kv.reshape(all_rows, 2 * HD)
    cuts = 8
    vmem = pl.BlockSpec(memory_space=pltpu.VMEM)
    smem = pl.BlockSpec(memory_space=pltpu.SMEM)
    hbm = pl.BlockSpec(memory_space=pl.ANY)
    relay = pltpu.VMEM((HALVES * hops, rows, chunk), jnp.bfloat16)
    dma = pltpu.SemaphoreType.DMA
    bf16, f32 = jnp.bfloat16, jnp.float32
    slot_shape = (ni * CAP, maxp) + kv_pool.shape[1:]
    home, arrive, got_pages = pl.pallas_call(
        functools.partial(layer_kernel, n, ni, chunks),
        out_shape=(
            jax.ShapeDtypeStruct((all_rows, share), bf16),
            jax.ShapeDtypeStruct((ni * slot_rows, share), bf16),
            jax.ShapeDtypeStruct(slot_shape, bf16),
        ),
        in_specs=[smem] * 5 + [hbm] * 4 + [vmem] * 3,
        out_specs=(vmem, vmem, hbm),
        scratch_shapes=[
            pltpu.VMEM((cuts, all_rows, width // cuts), bf16),
            pltpu.VMEM((cuts, width // cuts, columns), bf16),
            pltpu.VMEM(kv_pool.shape, bf16),
            pltpu.VMEM((n * chunks, columns, chunk), bf16),
            pltpu.VMEM((requests, pairs, HD), f32),
            pltpu.VMEM((requests, pairs, HD), f32),
            pltpu.VMEM((HALVES, rows, columns), bf16),
            pltpu.VMEM((HALVES, n * chunks, rows, chunk), f32),
            relay, relay, relay, relay,
            pltpu.VMEM(slot_shape, bf16),
            pltpu.VMEM((ni, slot_rows, all_rows), f32),
            pltpu.VMEM((ni, 2 * slot_rows, share // 2), bf16),
            pltpu.VMEM((ni, 2 * slot_rows, share // 2), bf16),
            pltpu.VMEM((2, requests, 16, HD), f32),
            dma((cuts,)), dma((cuts,)), dma, dma((n * chunks,)),
            dma((HALVES * hops,)), dma((HALVES * hops,)), dma((HALVES * hops,)), dma((HALVES * hops,)),
            dma((ni,)), dma((ni,)), dma((ni,)), dma((ni,)), dma((2,)),
        ],
        compiler_params=pltpu.CompilerParams(
            collective_id=0, has_side_effects=True, vmem_limit_bytes=60 * 1024 * 1024
        ),
    )(
        lengths, page_table.T, mig_req, mig_dest.reshape(-1), resume,
        hidden.reshape(-1, width), query_weight, kv_pool, output_weight, fresh, cosine, sine,
    )
    home = home.reshape(steps_n, requests, -1)
    arrival = arrive.reshape(steps_n, ni * CAP, -1)
    return emit(home, arrival, got_pages)


def solution(mesh):
    in_specs = (
        P(None, "inst", None),
        P(None, "tp"),
        P("tp", None),
        P("inst", None, None, "tp"),
        P(None, "inst", None, "tp"),
        P("inst"),
        P("inst", None),
        P("inst"),
        P("inst", None),
        P("inst"),
    )
    out_specs = (P(None, "inst", "tp"), P(None, "inst", "tp"), P("inst", None, None, None, "tp"))
    return jax.shard_map(local, mesh=mesh, in_specs=in_specs, out_specs=out_specs, check_vma=False)
```

```python
import functools

import jax
import jax.numpy as jnp
from jax import lax
from jax.experimental import pallas as pl
from jax.experimental.pallas import tpu as pltpu
from jax.sharding import PartitionSpec as P

HD = 128
CAP = 2
HALVES = 1


ROPE_BASE = 500000.0

MESH = pl.DeviceIdType.MESH


def turns(position, depth):
    half = depth // 2
    index = jnp.arange(depth, dtype=jnp.int32)
    inverse = ROPE_BASE ** (-(index % half).astype(jnp.float32) * 2.0 / depth)
    angles = position.astype(jnp.float32)[:, None] * inverse
    sign = jnp.where(index < half, -1.0, 1.0).astype(jnp.float32)
    return jnp.cos(angles), jnp.sin(angles) * sign


def emit_kernel(count, *refs):
    sources, targets = refs[:count], refs[count:2 * count]
    buffers = refs[2 * count:3 * count]
    in_sems, out_sems = refs[3 * count:]
    ins, outs = [], []
    for source, buffer, target in zip(sources, buffers, targets):
        for k in range(source.shape[0]):
            ins.append(pltpu.make_async_copy(source.at[k], buffer.at[k], in_sems.at[len(ins)]))
            outs.append(pltpu.make_async_copy(buffer.at[k], target.at[k], out_sems.at[len(outs)]))
    for copy in ins:
        copy.start()
    for first, second in zip(ins, outs):
        first.wait()
        second.start()
    for copy in outs:
        copy.wait()


def emit(*arrays):
    hbm = pl.BlockSpec(memory_space=pl.ANY)
    pieces = sum(x.shape[0] for x in arrays)
    return pl.pallas_call(
        functools.partial(emit_kernel, len(arrays)),
        out_shape=tuple(jax.ShapeDtypeStruct(x.shape, x.dtype) for x in arrays),
        in_specs=[hbm] * len(arrays),
        out_specs=(hbm,) * len(arrays),
        scratch_shapes=[pltpu.VMEM(x.shape, x.dtype) for x in arrays]
        + [pltpu.SemaphoreType.DMA((pieces,)), pltpu.SemaphoreType.DMA((pieces,))],
        compiler_params=pltpu.CompilerParams(vmem_limit_bytes=60 * 1024 * 1024),
    )(*arrays)


def layer_kernel(
    n, ni, chunks,
    lengths, table, mig_req, mig_dest, resume,
    hidden_ref, wq_ref, pool_ref, wo_ref, fresh_ref, cos_ref, sin_ref,
    home_ref, arrive_ref, got_ref,
    h_buf, wq_buf, pool, wo_buf, query, result, att, part, up_in, down_in, up_out, down_out,
    slots, select, leave, landed, fresh,
    h_sem, wq_sem, pool_sem, wo_sem,
    up_send, up_recv, down_send, down_recv, page_send, page_recv, row_send, row_recv, own_sem,
):
    z = lax.axis_index("tp")
    me = lax.axis_index("inst")
    cuts, depth, columns = wq_buf.shape
    requests, pairs, hd = query.shape
    groups = columns // hd
    steps_n = pairs // groups
    page = pool.shape[2]
    maxp = table.shape[0]
    leaving = mig_req.shape[0]
    some = requests // HALVES
    rows, width = part.shape[2:]
    hops = (n - 1) * chunks
    low = z < n // 2

    def h_copy(k):
        return pltpu.make_async_copy(
            hidden_ref.at[:, pl.ds(k * depth, depth)], h_buf.at[k], h_sem.at[k]
        )

    def wq_copy(k):
        return pltpu.make_async_copy(
            wq_ref.at[pl.ds(k * depth, depth)], wq_buf.at[k], wq_sem.at[k]
        )

    def block_of(k):
        return jnp.where(low, n - 1 - k // chunks, k // chunks)

    def wo_copy(k):
        column = (block_of(k) * chunks + k % chunks) * width
        return pltpu.make_async_copy(
            wo_ref.at[:, pl.ds(pl.multiple_of(column, width), width)], wo_buf.at[k], wo_sem.at[k]
        )

    pool_copy = pltpu.make_async_copy(pool_ref, pool, pool_sem)
    for k in range(cuts):
        h_copy(k).start()
        wq_copy(k).start()
    pool_copy.start()

    barrier = pltpu.get_barrier_semaphore()
    for k in range(1, ni):
        pl.semaphore_signal(
            barrier, inc=1, device_id={"inst": lax.rem(me + k, ni)}, device_id_type=MESH
        )

    @pl.when(z > 0)
    def _():
        pl.semaphore_signal(barrier, inc=1, device_id={"tp": z - 1}, device_id_type=MESH)

    @pl.when(z < n - 1)
    def _():
        pl.semaphore_signal(barrier, inc=1, device_id={"tp": z + 1}, device_id_type=MESH)

    slot_rows = CAP * steps_n
    shape = (slot_rows, HALVES * rows)
    slot_row = lax.broadcasted_iota(jnp.int32, shape, 0)
    row = lax.broadcasted_iota(jnp.int32, shape, 1)
    slot_step = slot_row % steps_n
    row_request = (row // rows) * some + row % some
    row_step = (row % rows) // some

    def fill(d, carry):
        count = jnp.int32(0)
        who = [jnp.int32(-1) for _ in range(CAP)]
        start = [jnp.int32(steps_n) for _ in range(CAP)]
        for k in range(leaving):
            match = mig_dest[k] == d
            for c in range(CAP):
                take = match & (count == c)
                who[c] = jnp.where(take, mig_req[k], who[c])
                start[c] = jnp.where(take, resume[k], start[c])
            count = count + match.astype(jnp.int32)
        chosen = jnp.full(shape, -1, jnp.int32)
        first = jnp.full(shape, steps_n, jnp.int32)
        for c in range(CAP):
            chosen = jnp.where(slot_row // steps_n == c, who[c], chosen)
            first = jnp.where(slot_row // steps_n == c, start[c], first)
            for p in range(maxp):
                pages = pool[table[p, jnp.maximum(who[c], 0)]]
                slots[d * CAP + c, p] = jnp.where(who[c] >= 0, pages, jnp.zeros_like(pages))
        hit = (row_request == chosen) & (row_step == slot_step) & (slot_step >= first)
        select[d] = hit.astype(jnp.float32)
        return carry

    def page_copy(k):
        to = lax.rem(me + k, ni)
        return pltpu.make_async_remote_copy(
            src_ref=slots.at[pl.ds(to * CAP, CAP)],
            dst_ref=got_ref.at[pl.ds(me * CAP, CAP)],
            send_sem=page_send.at[k],
            recv_sem=page_recv.at[k],
            device_id={"inst": to},
            device_id_type=MESH,
        )

    own_pages = pltpu.make_async_copy(
        slots.at[pl.ds(me * CAP, CAP)], got_ref.at[pl.ds(me * CAP, CAP)], own_sem.at[0]
    )
    total = jnp.zeros((h_buf.shape[1], columns), jnp.float32)
    for k in range(cuts):
        h_copy(k).wait()
        wq_copy(k).wait()
        if k == cuts - 2:
            for c in range(n * chunks):
                wo_copy(c).start()
        total = total + jnp.dot(h_buf[k], wq_buf[k], preferred_element_type=jnp.float32)
    for g in range(groups):
        head = total[:, g * hd:(g + 1) * hd]
        head = head * cos_ref[...] + pltpu.roll(head, hd // 2, 1) * sin_ref[...]
        for s in range(steps_n):
            query[:, s * groups + g, :] = head[s * requests:(s + 1) * requests]

    pl.semaphore_wait(barrier, ni - 1 + (z > 0).astype(jnp.int32) + (z < n - 1).astype(jnp.int32))

    fresh[...] = jnp.zeros_like(fresh)
    for u in range(steps_n):
        for kind in range(2):
            fresh[kind, :, u, :] = fresh_ref[
                u * requests:(u + 1) * requests, kind * hd:(kind + 1) * hd
            ].astype(jnp.float32)

    pool_copy.wait()
    batch = 8
    old = maxp * page
    span = old + page
    column = lax.broadcasted_iota(jnp.int32, (batch * pairs, span), 1)
    step = (lax.broadcasted_iota(jnp.int32, (batch * pairs, span), 0) % pairs) // groups
    newer = (column >= old) & (column - old <= step)
    scale = hd ** (-0.5)
    empty = jnp.zeros((page - fresh.shape[2], hd), jnp.bfloat16)

    def stacked(r, kind):
        return jnp.concatenate(
            [pool[table[p, r], kind] for p in range(maxp)]
            + [fresh[kind, r].astype(jnp.bfloat16), empty],
            axis=0,
        )

    def several(i, carry):
        first = i * batch
        scores = jnp.concatenate(
            [
                lax.dot_general(
                    query[first + k].astype(jnp.bfloat16), stacked(first + k, 0),
                    (((1,), (1,)), ((), ())), preferred_element_type=jnp.float32,
                )
                for k in range(batch)
            ],
            axis=0,
        ) * scale
        length = jnp.concatenate(
            [jnp.full((pairs, span), lengths[first + k], jnp.int32) for k in range(batch)], axis=0
        )
        scores = jnp.where(newer | (column < length), scores, -1e30)
        weight = jnp.exp(scores - jnp.max(scores, axis=1, keepdims=True))
        probs = (weight / jnp.sum(weight, axis=1, keepdims=True)).astype(jnp.bfloat16)
        for k in range(batch):
            result[first + k] = jnp.dot(
                probs[k * pairs:(k + 1) * pairs], stacked(first + k, 1),
                preferred_element_type=jnp.float32,
            )
        return carry

    def up_copy(j):
        return pltpu.make_async_remote_copy(
            src_ref=up_out.at[j], dst_ref=up_in.at[j],
            send_sem=up_send.at[j], recv_sem=up_recv.at[j],
            device_id={"tp": jnp.minimum(z + 1, n - 1)}, device_id_type=MESH,
        )

    def down_copy(j):
        return pltpu.make_async_remote_copy(
            src_ref=down_out.at[j], dst_ref=down_in.at[j],
            send_sem=down_send.at[j], recv_sem=down_recv.at[j],
            device_id={"tp": jnp.maximum(z - 1, 0)}, device_id_type=MESH,
        )

    for h in range(HALVES):
        lax.fori_loop(h * some // batch, (h + 1) * some // batch, several, 0)
        for s in range(steps_n):
            for g in range(groups):
                att[h, s * some:(s + 1) * some, g * hd:(g + 1) * hd] = result[
                    h * some:(h + 1) * some, s * groups + g, :
                ].astype(jnp.bfloat16)

        def compute(k, carry, h=h):
            if h == 0:
                wo_copy(k).wait()
            value = jnp.dot(att[h], wo_buf[k], preferred_element_type=jnp.float32)
            part[h, block_of(k) * chunks + k % chunks] = value

            @pl.when((z == 0) & (k < hops))
            def _():
                up_out[h * hops + k] = value.astype(jnp.bfloat16)
                up_copy(h * hops + k).start()

            @pl.when((z == n - 1) & (k < hops))
            def _():
                down_out[h * hops + k] = value.astype(jnp.bfloat16)
                down_copy(h * hops + k).start()

            return carry

        lax.fori_loop(0, n * chunks, compute, 0)
        if h == 0:
            lax.fori_loop(0, ni, fill, 0)
            for k in range(1, ni):
                page_copy(k).start()
            own_pages.start()

    selection = select[...].reshape(ni * slot_rows, HALVES * rows).astype(jnp.bfloat16)
    lane_row = lax.broadcasted_iota(jnp.int32, (rows, hd), 0)
    half = chunks // 2
    stays = []
    for h in range(HALVES):
        kept = jnp.ones((rows, hd), jnp.int32)
        for k in range(leaving):
            gone = (lane_row % some + h * some == mig_req[k]) & (lane_row // some >= resume[k])
            kept = jnp.where(gone, 0, kept)
        stays.append(jnp.concatenate([kept] * (width // hd), axis=1))
    up_lag = jnp.maximum(z - 1, 0)
    down_lag = jnp.maximum(n - 2 - z, 0)
    for h in range(HALVES):

        def relay(j, carry, h=h):
            ju = j - up_lag
            jd = j - down_lag

            @pl.when((z > 0) & (ju >= 0) & (ju < (n - z) * chunks))
            def _():
                up_copy(h * hops + ju).wait_recv()
                spot = (n - 1 - ju // chunks) * chunks + ju % chunks
                value = part[h, spot] + up_in[h * hops + ju].astype(jnp.float32)

                @pl.when(ju < (n - 1 - z) * chunks)
                def _():
                    up_out[h * hops + ju] = value.astype(jnp.bfloat16)
                    up_copy(h * hops + ju).start()

                @pl.when(ju >= (n - 1 - z) * chunks)
                def _():
                    part[h, spot] = value

            @pl.when((z < n - 1) & (jd >= 0) & (jd < (z + 1) * chunks))
            def _():
                down_copy(h * hops + jd).wait_recv()
                value = part[h, jd] + down_in[h * hops + jd].astype(jnp.float32)

                @pl.when(jd < z * chunks)
                def _():
                    down_out[h * hops + jd] = value.astype(jnp.bfloat16)
                    down_copy(h * hops + jd).start()

                @pl.when(jd >= z * chunks)
                def _():
                    part[h, jd] = value

            return carry

        lax.fori_loop(0, hops + n - 2, relay, 0)

    for c in range(half):
        pieces = []
        for d in (c, c + half):
            mines = []
            for h in range(HALVES):
                mine = part[h, z * chunks + d].astype(jnp.bfloat16)
                mines.append(mine)
                kept = jnp.where(stays[h] > 0, mine.astype(jnp.float32), 0.0).astype(jnp.bfloat16)
                for s in range(steps_n):
                    home_ref[
                        s * requests + h * some:s * requests + (h + 1) * some,
                        d * width:(d + 1) * width,
                    ] = kept[s * some:(s + 1) * some]
            moved = jnp.dot(
                selection, jnp.concatenate(mines, axis=0), preferred_element_type=jnp.float32
            )
            pieces.append(moved.reshape(ni, slot_rows, width))
        leave[:, :, c * width:(c + 1) * width] = jnp.concatenate(pieces, axis=1).astype(jnp.bfloat16)

    def row_copy(k):
        to = lax.rem(me + k, ni)
        return pltpu.make_async_remote_copy(
            src_ref=leave.at[to],
            dst_ref=landed.at[me],
            send_sem=row_send.at[k],
            recv_sem=row_recv.at[k],
            device_id={"inst": to},
            device_id_type=MESH,
        )

    own_rows = pltpu.make_async_copy(leave.at[me], landed.at[me], own_sem.at[1])
    for k in range(1, ni):
        row_copy(k).start()
    own_rows.start()

    for h in range(HALVES):

        def drain(j, carry, h=h):
            @pl.when((z < n - 1) & (j < (n - 1 - z) * chunks))
            def _():
                up_copy(h * hops + j).wait_send()

            @pl.when((z > 0) & (j < z * chunks))
            def _():
                down_copy(h * hops + j).wait_send()

            return carry

        lax.fori_loop(0, hops, drain, 0)
    for k in range(1, ni):
        row_copy(k).wait()
    own_rows.wait()
    arrivals = landed[...].reshape(2 * ni * slot_rows, landed.shape[2])
    shape = (ni * slot_rows, 2 * ni * slot_rows)
    out_row = lax.broadcasted_iota(jnp.int32, shape, 0)
    in_row = lax.broadcasted_iota(jnp.int32, shape, 1)
    out_slot = out_row % (ni * CAP)
    place = (out_slot // CAP) * 2 * slot_rows + (out_slot % CAP) * steps_n + out_row // (ni * CAP)
    side = landed.shape[2]
    for d in range(2):
        order = (in_row == place + d * slot_rows).astype(jnp.float32).astype(jnp.bfloat16)
        arrive_ref[:, d * side:(d + 1) * side] = jnp.dot(
            order, arrivals, preferred_element_type=jnp.float32
        ).astype(jnp.bfloat16)
    for k in range(1, ni):
        page_copy(k).wait()
    own_pages.wait()


def local(
    hidden,
    query_weight,
    output_weight,
    kv_pool,
    new_kv,
    lengths,
    page_table,
    mig_req,
    mig_dest,
    resume,
):
    steps_n, requests, width = hidden.shape
    n = lax.axis_size("tp")
    ni = lax.axis_size("inst")
    columns = query_weight.shape[1]
    pairs = steps_n * (columns // HD)
    maxp = page_table.shape[1]
    all_rows = steps_n * requests
    rows = all_rows // HALVES
    share = output_weight.shape[1] // n
    chunk = min(512, share // 2)
    chunks = share // chunk
    hops = (n - 1) * chunks
    slot_rows = CAP * steps_n
    position = lengths[None, :] + jnp.arange(steps_n, dtype=jnp.int32)[:, None]
    cosine, sine = turns(position.reshape(-1), HD)
    fresh = new_kv.reshape(all_rows, 2 * HD)
    cuts = 8
    vmem = pl.BlockSpec(memory_space=pltpu.VMEM)
    smem = pl.BlockSpec(memory_space=pltpu.SMEM)
    hbm = pl.BlockSpec(memory_space=pl.ANY)
    relay = pltpu.VMEM((HALVES * hops, rows, chunk), jnp.bfloat16)
    dma = pltpu.SemaphoreType.DMA
    bf16, f32 = jnp.bfloat16, jnp.float32
    slot_shape = (ni * CAP, maxp) + kv_pool.shape[1:]
    home, arrive, got_pages = pl.pallas_call(
        functools.partial(layer_kernel, n, ni, chunks),
        out_shape=(
            jax.ShapeDtypeStruct((all_rows, share), bf16),
            jax.ShapeDtypeStruct((ni * slot_rows, share), bf16),
            jax.ShapeDtypeStruct(slot_shape, bf16),
        ),
        in_specs=[smem] * 5 + [hbm] * 4 + [vmem] * 3,
        out_specs=(vmem, vmem, hbm),
        scratch_shapes=[
            pltpu.VMEM((cuts, all_rows, width // cuts), bf16),
            pltpu.VMEM((cuts, width // cuts, columns), bf16),
            pltpu.VMEM(kv_pool.shape, bf16),
            pltpu.VMEM((n * chunks, columns, chunk), bf16),
            pltpu.VMEM((requests, pairs, HD), f32),
            pltpu.VMEM((requests, pairs, HD), f32),
            pltpu.VMEM((HALVES, rows, columns), bf16),
            pltpu.VMEM((HALVES, n * chunks, rows, chunk), f32),
            relay, relay, relay, relay,
            pltpu.VMEM(slot_shape, bf16),
            pltpu.VMEM((ni, slot_rows, all_rows), f32),
            pltpu.VMEM((ni, 2 * slot_rows, share // 2), bf16),
            pltpu.VMEM((ni, 2 * slot_rows, share // 2), bf16),
            pltpu.VMEM((2, requests, 16, HD), f32),
            dma((cuts,)), dma((cuts,)), dma, dma((n * chunks,)),
            dma((HALVES * hops,)), dma((HALVES * hops,)), dma((HALVES * hops,)), dma((HALVES * hops,)),
            dma((ni,)), dma((ni,)), dma((ni,)), dma((ni,)), dma((2,)),
        ],
        compiler_params=pltpu.CompilerParams(
            collective_id=0, has_side_effects=True, vmem_limit_bytes=60 * 1024 * 1024
        ),
    )(
        lengths, page_table.T, mig_req, mig_dest.reshape(-1), resume,
        hidden.reshape(-1, width), query_weight, kv_pool, output_weight, fresh, cosine, sine,
    )
    home = home.reshape(steps_n, requests, -1)
    arrival = arrive.reshape(steps_n, ni * CAP, -1)
    return emit(home, arrival, got_pages)


def solution(mesh):
    in_specs = (
        P(None, "inst", None),
        P(None, "tp"),
        P("tp", None),
        P("inst", None, None, "tp"),
        P(None, "inst", None, "tp"),
        P("inst"),
        P("inst", None),
        P("inst"),
        P("inst", None),
        P("inst"),
    )
    out_specs = (P(None, "inst", "tp"), P(None, "inst", "tp"), P("inst", None, None, None, "tp"))
    return jax.shard_map(local, mesh=mesh, in_specs=in_specs, out_specs=out_specs, check_vma=False)
```
